768 devices in a mesh: owner: 32 (over y, x), rep: 24 (over z, core).
Axes of the slice: x: 4, y: 8, z: 12, core: 2. Of those that a mesh axis runs over, the one named last changes fastest.
Arguments:
- cotangent: bfloat16 [589824, 256], P(('owner', 'rep')), may hold values from -6 to 6
- pre_two: bfloat16 [589824, 256], P(('owner', 'rep')), may hold values from -6 to 6
- pre_one: bfloat16 [589824, 256], P(('owner', 'rep')), may hold values from -6 to 6
- message_two: bfloat16 [589824, 256], P(('owner', 'rep')), may hold values from -6 to 6
- message_one: bfloat16 [589824, 256], P(('owner', 'rep')), may hold values from -6 to 6
- users_zero: bfloat16 [589824, 256], P(('owner', 'rep')), may hold values from -6 to 6
- w_self: bfloat16 [2, 256, 256], replicated, may hold values from -0.375 to 0.375
- w_inter: bfloat16 [2, 256, 256], replicated, may hold values from -0.375 to 0.375
- adjacency: bfloat16 [3072, 256, 256], P(('owner', 'rep')), may hold values from 0 to 0.125
- tile_user: int32 [3072], P(('owner', 'rep')), may hold values from 0 to 2
- counts: int32 [3072], P(('owner', 'rep')), may hold values from 1 to 256
- dest: int32 [24576, 1], P(('owner', 'rep')), may hold values from 0 to 31; in each aligned block of 32 rows (0 to 31, 32 to 63, ...) at most 2 rows name the same one
- item_block: int32 [24576], P(('owner', 'rep')), may hold values from 0 to 31
Outputs:
- user_grad: bfloat16 [589824, 256], P(('owner', 'rep'))
- item_grad_one: bfloat16 [786432, 256], P(('owner', 'rep'))
- item_grad_zero: bfloat16 [786432, 256], P(('owner', 'rep'))
- w_self_grad: float32 [2, 256, 256], replicated
- w_inter_grad: float32 [2, 256, 256], replicated
The draws below stay inside these ranges and needn't reach their ends.
Inputs may be any that keep to these rules, and one draw needn't show every extreme that they name: `dest`: among the 32 row blocks of one device no owner index appears more than 2 times, and in every draw some owner is named exactly 2 times by some device.
All inputs are finite; a program needn't handle non-finite values.
Results may differ from the reference program's by a relative error of at most 0.009.
Values may be sent and summed in bfloat16 or wider, within the bound.
No kernel may reach another device: no remote copies, remote signals or barrier semaphores. Data moves between devices by JAX's collectives and lax.ppermute only.
A program may use at most 32 MiB of HBM per device.

```python
import math
import jax
import jax.numpy as jnp
import numpy as np
from jax import lax

FEAT = 256
UBS = 256
IBS = 256
RB = 32
K = 4
UB = 3
IBD = 32
RBT = 8
CAP = 2
USERS = 589824
TILES = 3072
N_OWNER = 32
N_REP = 24


def set_ends(array, own_key, smallest, high):
    place = [jax.random.randint(jax.random.fold_in(own_key, axis), (), 0, length) for axis, length in enumerate(array.shape)]
    widest = array.shape.index(max(array.shape))
    beside = place[:widest] + [(place[widest] + 1) % array.shape[widest]] + place[widest + 1:]
    return array.at[tuple(place)].set(smallest).at[tuple(beside)].set(high)


def shard_levels(key, dims, cuts, smallest, top_value):
    def one(axis_at, parts):
        steps = jax.random.uniform(jax.random.fold_in(jax.random.fold_in(key, 6), axis_at), (parts,), jnp.float32, smallest / len(cuts), top_value / len(cuts))
        return jnp.repeat(jnp.exp(steps), dims[axis_at] // parts).reshape((-1,) + (1,) * (len(dims) - axis_at - 1))

    gain = one(*cuts[0])
    for cut in cuts[1:]:
        gain = gain * one(*cut)
    return gain


def deal_out(rng, own, number, rows, count, top, reach, skew):
    sequence = jax.random.permutation(rng, count)
    heavy_load, ordinary = portions_of(count, rows * top, reach, skew, True), portions_of(count, rows * top, reach, skew, False)
    places = jnp.arange(count)

    def named(tallies, turn):
        used = int((tallies > 0).sum())
        fixed = max(1, used // 4)
        passed = fixed + (places - fixed + turn * (used - fixed)) % max(1, count - fixed)
        return jnp.zeros((count,), jnp.int32).at[sequence[jnp.where(places < fixed, places, passed)]].set(jnp.asarray(tallies, jnp.int32))

    tallies = jnp.where(number % 4 == 0, named(heavy_load, number // 4), named(ordinary, number - number // 4 - 1))
    mixed = jax.random.permutation(jax.random.fold_in(own, 3), count)
    giver, sink = mixed[0:count // 2 * 2:2], mixed[1:count // 2 * 2:2]
    slack = jnp.minimum(tallies[giver] - 1, reach - tallies[sink]) // 2
    slack = jnp.where((giver == sequence[0]) | (sink == sequence[0]) | (tallies[sink] == 0), 0, jnp.maximum(slack, 0))
    passed = jax.random.randint(jax.random.fold_in(own, 4), (count // 2,), 0, 1 << 20) % (slack + 1)
    tallies = tallies.at[giver].add(-passed).at[sink].add(passed)
    members = jnp.searchsorted(jnp.cumsum(tallies), jnp.arange(rows * top), side="right").astype(jnp.int32)
    listing = members.reshape(top, rows).T
    listing = listing[jax.random.permutation(jax.random.fold_in(own, 1), rows)]
    turn = jax.random.randint(jax.random.fold_in(own, 2), (rows, 1), 0, top)
    return jnp.take_along_axis(listing, (jnp.arange(top)[None, :] + turn) % top, axis=1)


def portions_of(count, total, bound, slope, full):
    loads = [(1 << 20) // math.isqrt(grade ** slope) + 1 for grade in range(1, count + 1)]
    largest = bound if full else min(bound, max(-(-total // count), total * loads[0] // sum(loads)))
    least = 1 if total - largest >= count - 1 else 0
    holding, surplus = [largest] + [least] * (count - 1), total - largest - least * (count - 1)
    while surplus > 0:
        free = [i for i in range(1, count) if holding[i] < largest] or [i for i in range(1, count) if holding[i] < bound]
        mass, left = sum([loads[i] for i in free]), surplus
        for i in free:
            addition = min(bound - holding[i], max(1, left * loads[i] // mass), surplus)
            holding[i] = holding[i] + addition
            surplus = surplus - addition
    return np.array(holding)


def bell_draw(stream_key, extent, spread, most, cuts=(), kind=jnp.bfloat16):
    gain = shard_levels(stream_key, extent, cuts, -0.22, 0.18) if cuts else 1.0
    values = jax.random.normal(stream_key, extent, jnp.float32) * spread * gain
    return jnp.minimum(jnp.maximum(values, -most), most).astype(kind)


def setup_inputs(seed: int = 0) -> dict:
    keys = jax.random.split(jax.random.key(seed), 14)
    cotangent = bell_draw(keys[0], (USERS, FEAT), 1.0, 6.0, ((0, 768),))
    pre_two = bell_draw(keys[1], (USERS, FEAT), 1.0, 6.0, ((0, 768),))
    pre_one = bell_draw(keys[2], (USERS, FEAT), 1.0, 6.0, ((0, 768),))
    message_two = bell_draw(keys[3], (USERS, FEAT), 1.0, 6.0, ((0, 768),))
    message_one = bell_draw(keys[4], (USERS, FEAT), 1.0, 6.0, ((0, 768),))
    users_zero = bell_draw(keys[5], (USERS, FEAT), 1.0, 6.0, ((0, 768),))
    w_self = bell_draw(keys[6], (2, FEAT, FEAT), FEAT ** -0.5, 0.375)
    w_inter = bell_draw(keys[7], (2, FEAT, FEAT), FEAT ** -0.5, 0.375)
    adjacency = jnp.clip(0.125 * jax.random.uniform(keys[8], (TILES, UBS, IBS), jnp.float32) ** shard_levels(keys[8], (TILES, UBS, IBS), ((0, 768),), -0.2, 0.2), 0.0, 0.125).astype(jnp.bfloat16)
    tile_user = set_ends(jax.random.randint(keys[9], (TILES,), 0, UB), jax.random.fold_in(keys[9], 1), 0, UB - 1).astype(jnp.int32)
    counts = set_ends(jax.random.randint(keys[10], (TILES,), 1, IBS + 1), jax.random.fold_in(keys[10], 1), 1, IBS).astype(jnp.int32)
    dest_keys = jax.random.split(jax.random.fold_in(keys[11], 1), (TILES * RBT) // (K * RBT))
    dest_turns = jax.random.permutation(jax.random.fold_in(keys[11], 3), (TILES * RBT) // (K * RBT))
    dest = jax.vmap(lambda own, number: deal_out(jax.random.fold_in(keys[11], 2), own, number, K * RBT, N_OWNER, 1, CAP, 2))(dest_keys, dest_turns).reshape((TILES * RBT, 1))
    item_block = set_ends(jax.random.randint(keys[12], (TILES * RBT,), 0, IBD), jax.random.fold_in(keys[12], 1), 0, IBD - 1).astype(jnp.int32)
    return dict(cotangent=cotangent, pre_two=pre_two, pre_one=pre_one, message_two=message_two, message_one=message_one, users_zero=users_zero, w_self=w_self, w_inter=w_inter, adjacency=adjacency, tile_user=tile_user, counts=counts, dest=dest, item_block=item_block)


SLOPE = 0.2


def layer_back(gradient, pre_act, message, previous, w_self, w_inter):
    deltas = (gradient * jnp.where(pre_act > 0, 1.0, SLOPE)).astype(jnp.bfloat16)
    summed = (message.astype(jnp.float32) + previous.astype(jnp.float32)).astype(jnp.bfloat16)
    product = (message.astype(jnp.float32) * previous.astype(jnp.float32)).astype(jnp.bfloat16)
    grad_self = jnp.dot(summed.T, deltas, preferred_element_type=jnp.float32)
    grad_inter = jnp.dot(product.T, deltas, preferred_element_type=jnp.float32)
    back_self = jnp.dot(deltas, w_self.T, preferred_element_type=jnp.float32)
    back_inter = jnp.dot(deltas, w_inter.T, preferred_element_type=jnp.float32)
    d_message = (back_self + back_inter * previous.astype(jnp.float32)).astype(jnp.bfloat16)
    d_previous = back_self + back_inter * message.astype(jnp.float32)
    return grad_self, grad_inter, d_message, d_previous


def item_adjoint(d_message, masked_adj, tile_user, dest, item_block):
    devices = N_OWNER * N_REP
    msg_dev = d_message.reshape(devices, UB, UBS, FEAT)
    adj_dev = masked_adj.reshape(devices, K, UBS, IBS)
    users_dev = tile_user.reshape(devices, K)

    def per_device(pieces):
        adj_one, users_one, msg_one = pieces
        picked = msg_one[users_one]
        partial_value = jnp.einsum('kui,kuf->kif', adj_one.astype(jnp.float32), picked.astype(jnp.float32))
        return partial_value.astype(jnp.bfloat16).reshape(K * RBT, RB, FEAT)

    partials = lax.map(per_device, (adj_dev, users_dev, msg_dev)).reshape(devices * K * RBT, RB, FEAT)
    device = jnp.arange(devices * K * RBT, dtype=jnp.int32) // (K * RBT)
    segment = ((dest[:, 0] * N_REP + device % N_REP) * IBD + item_block).astype(jnp.int32)
    total = jax.ops.segment_sum(partials.astype(jnp.float32), segment, num_segments=devices * IBD)
    return total.reshape(devices * IBD * RB, FEAT).astype(jnp.bfloat16)


def reference(cotangent, pre_two, pre_one, message_two, message_one, users_zero, w_self, w_inter, adjacency, tile_user, counts, dest, item_block):
    live_cols = jnp.arange(IBS, dtype=jnp.int32)[None, :] < counts[:, None]
    masked_adj = jnp.where(live_cols[:, None, :], adjacency, jnp.zeros((), jnp.bfloat16))
    one_f = pre_one.astype(jnp.float32)
    users_one = jnp.where(one_f > 0, one_f, SLOPE * one_f).astype(jnp.bfloat16)
    self_two, inter_two, msg_two, prev_two = layer_back(cotangent.astype(jnp.float32), pre_two, message_two, users_one, w_self[1], w_inter[1])
    self_one, inter_one, msg_one, prev_one = layer_back(prev_two, pre_one, message_one, users_zero, w_self[0], w_inter[0])
    item_one = item_adjoint(msg_two, masked_adj, tile_user, dest, item_block)
    item_zero = item_adjoint(msg_one, masked_adj, tile_user, dest, item_block)
    return (prev_one.astype(jnp.bfloat16), item_one, item_zero, jnp.stack([self_one, self_two]), jnp.stack([inter_one, inter_two]))
```

```python
import functools

import jax
import jax.numpy as jnp
from jax import lax
from jax.experimental import pallas as pl
from jax.experimental.pallas import tpu as pltpu
from jax.sharding import PartitionSpec as P

BF = jnp.bfloat16
F32 = jnp.float32
SLOPE = 0.2
RB = 32
FEAT = 256
HALF = 128
BLK = 256
OWNERS = 32
TRASH = 32
VMEM = pl.BlockSpec(memory_space=pltpu.VMEM)
SMEM = pl.BlockSpec(memory_space=pltpu.SMEM)
PARAMS = pltpu.CompilerParams(vmem_limit_bytes=40 * 1024 * 1024)


def tdot(a, b):
    return lax.dot_general(a, b, (((0,), (0,)), ((), ())), preferred_element_type=F32)


def dot_t(a, b):
    return lax.dot_general(a, b, (((1,), (1,)), ((), ())), preferred_element_type=F32)


def layer_math(layer, grad_ref, pre_ref, msg_ref, prev_ref, ws_ref, wi_ref, dprev_ref, delta_s, sum_s, prod_s, dmsg_s):
    for b in range(grad_ref.shape[0] // BLK):
        rows = pl.ds(b * BLK, BLK)
        pre = pre_ref[rows, :].astype(F32)
        deltas = (grad_ref[rows, :].astype(F32) * jnp.where(pre > 0, 1.0, SLOPE)).astype(BF)
        prev = prev_ref[rows, :].astype(F32)
        if layer == 1:
            prev = jnp.where(prev > 0, prev, SLOPE * prev).astype(BF).astype(F32)
        msg = msg_ref[rows, :].astype(F32)
        delta_s[rows, :] = deltas
        sum_s[rows, :] = (msg + prev).astype(BF)
        prod_s[rows, :] = (msg * prev).astype(BF)
        back_self = dot_t(deltas, ws_ref[layer])
        back_inter = dot_t(deltas, wi_ref[layer])
        dmsg_s[rows, :] = (back_self + back_inter * prev).astype(BF)
        dprev_ref[rows, :] = (back_self + back_inter * msg).astype(dprev_ref.dtype)


def split_grads(delta_s, sum_s, prod_s, keep_ref, send_ref):
    grad_self = tdot(sum_s[...], delta_s[...])
    grad_inter = tdot(prod_s[...], delta_s[...])
    core = lax.rem(lax.axis_index("rep"), 2)
    even = core == 0
    keep_ref[...] = jnp.where(even, grad_self, grad_inter)
    send_ref[...] = jnp.where(even, grad_inter, grad_self)


def rank_blocks(dest_ref, rank_s, seen_s):
    for o in range(OWNERS):
        seen_s[o] = 0
    for j in range(dest_ref.shape[0]):
        o = dest_ref[j, 0]
        rank_s[j] = seen_s[o]
        seen_s[o] = seen_s[o] + 1


def tile_terms(adj_ref, user_ref, count_ref, dmsg_s, store):
    for t in range(adj_ref.shape[0]):
        start = pl.multiple_of(user_ref[t] * BLK, BLK)
        part = tdot(adj_ref[t], dmsg_s[pl.ds(start, BLK), :])
        live = lax.broadcasted_iota(jnp.int32, part.shape, 0) < count_ref[t]
        part = jnp.where(live, part, 0.0).astype(BF)
        for b in range(part.shape[0] // RB):
            store(t * (part.shape[0] // RB) + b, part[b * RB : (b + 1) * RB, :])


def two_kernel(user_ref, count_ref, dest_ref, item_ref, cot_ref, pre_ref, msg_ref, one_ref, ws_ref, wi_ref, adj_ref,
               dprev_ref, a_ref, second_ref, keep_ref, send_ref, delta_s, sum_s, prod_s, dmsg_s, rank_s, seen_s, tab_s):
    rank_blocks(dest_ref, rank_s, seen_s)
    for i in range(2 * OWNERS):
        tab_s[i] = TRASH
    for j in range(dest_ref.shape[0]):
        tab_s[2 * dest_ref[j, 0] + rank_s[j]] = item_ref[j]
    a_ref[...] = jnp.zeros_like(a_ref)
    second_ref[...] = jnp.zeros_like(second_ref)
    top = lax.broadcasted_iota(jnp.int32, (16, HALF), 0) < 8
    for o in range(OWNERS):
        a_ref[o, 64:80, :] = jnp.where(top, tab_s[2 * o], tab_s[2 * o + 1]).astype(F32).astype(BF)
    layer_math(1, cot_ref, pre_ref, msg_ref, one_ref, ws_ref, wi_ref, dprev_ref, delta_s, sum_s, prod_s, dmsg_s)

    def store(j, block):
        o = dest_ref[j, 0]

        @pl.when(rank_s[j] == 0)
        def _():
            a_ref[o, 0:32, :] = block[:, :HALF]
            a_ref[o, 32:64, :] = block[:, HALF:]

        @pl.when(rank_s[j] != 0)
        def _():
            second_ref[o, 0:32, :] = block[:, :HALF]
            second_ref[o, 32:64, :] = block[:, HALF:]

    tile_terms(adj_ref, user_ref, count_ref, dmsg_s, store)
    split_grads(delta_s, sum_s, prod_s, keep_ref, send_ref)


def one_kernel(user_ref, count_ref, dest_ref, grad_ref, pre_ref, msg_ref, zero_ref, ws_ref, wi_ref, adj_ref,
               user_grad_ref, c_ref, d_ref, keep_ref, send_ref, delta_s, sum_s, prod_s, dmsg_s, rank_s, seen_s):
    rank_blocks(dest_ref, rank_s, seen_s)
    c_ref[...] = jnp.zeros_like(c_ref)
    d_ref[...] = jnp.zeros_like(d_ref)
    layer_math(0, grad_ref, pre_ref, msg_ref, zero_ref, ws_ref, wi_ref, user_grad_ref, delta_s, sum_s, prod_s, dmsg_s)
    split_grads(delta_s, sum_s, prod_s, keep_ref, send_ref)

    def store(j, block):
        o = dest_ref[j, 0]

        @pl.when(rank_s[j] == 0)
        def _():
            c_ref[o, 0:32, :] = block[:, :HALF]
            c_ref[o, 32:64, :] = block[:, HALF:]

        @pl.when(rank_s[j] != 0)
        def _():
            c_ref[o, 64:96, :] = block[:, :HALF]
            d_ref[o, :, :] = block[:, HALF:]

    tile_terms(adj_ref, user_ref, count_ref, dmsg_s, store)


def pack_kernel(second_ref, keep2_ref, got2_ref, keep1_ref, got1_ref, b_ref):
    for o in range(OWNERS):
        b_ref[o, 0:64, :] = second_ref[o]
        rows = slice(8 * o, 8 * o + 8)
        for at, keep_ref, got_ref in ((64, keep2_ref, got2_ref), (80, keep1_ref, got1_ref)):
            total = keep_ref[rows, :] + got_ref[rows, :]
            b_ref[o, at : at + 16, :] = jnp.concatenate([total[:, :HALF], total[:, HALF:]], axis=0).astype(BF)


def chunk_kernel(b_ref, total_ref):
    acc = b_ref[0, 64:96, :].astype(F32)
    for s in range(1, OWNERS):
        acc = acc + b_ref[s, 64:96, :].astype(F32)
    total_ref[...] = acc


def collect_kernel(cuts, index_ref, *refs):
    *in_refs, out_ref, acc_s = refs
    acc_s[...] = jnp.zeros_like(acc_s)

    def body(s, carry):
        for ref, pieces in zip(in_refs, cuts):
            for slot, at, to, rows in pieces:
                i = index_ref[2 * s + slot]
                acc_s[i, to : to + rows, :] += ref[s, at : at + rows, :].astype(F32)
        return carry

    lax.fori_loop(0, OWNERS, body, 0, unroll=4)
    for i in range(TRASH):
        out_ref[RB * i : RB * i + RB, :HALF] = acc_s[i, 0:32, :].astype(BF)
        out_ref[RB * i : RB * i + RB, HALF:] = acc_s[i, 32:64, :].astype(BF)


def unpack_kernel(mine_ref, other_ref, self_ref, inter_ref):
    even = lax.rem(lax.axis_index("rep"), 2) == 0
    for o in range(OWNERS):
        mine = mine_ref[o, 32:64, :].astype(F32)
        other = other_ref[o].astype(F32)
        a = jnp.where(even, mine, other)
        b = jnp.where(even, other, mine)
        rows = slice(8 * o, 8 * o + 8)
        for ref, value in ((self_ref, a), (inter_ref, b)):
            ref[1, rows, :HALF] = value[0:8]
            ref[1, rows, HALF:] = value[8:16]
            ref[0, rows, :HALF] = value[16:24]
            ref[0, rows, HALF:] = value[24:32]


def call(kernel, outs, in_specs, scratch=(), **cost):
    return pl.pallas_call(
        kernel,
        out_shape=[jax.ShapeDtypeStruct(s, d) for s, d in outs],
        in_specs=in_specs,
        out_specs=[VMEM] * len(outs),
        scratch_shapes=list(scratch),
        compiler_params=PARAMS,
        cost_estimate=pl.CostEstimate(transcendentals=0, **cost),
    )


def local(cotangent, pre_two, pre_one, message_two, message_one, users_zero, w_self, w_inter, adjacency, tile_user,
          counts, dest, item_block):
    users = cotangent.shape[0]
    reps = lax.axis_size("rep")
    swap = [(i, i ^ 1) for i in range(reps)]

    def along_z(step):
        return [(2 * z + c, 2 * step(z) + c) for z in range(reps // 2) for c in range(2)]

    def to_owners(x):
        return lax.all_to_all(x, "owner", split_axis=0, concat_axis=0, tiled=True)

    scratch = [pltpu.VMEM((users, FEAT), BF)] * 4 + [pltpu.SMEM((OWNERS,), jnp.int32)] * 2
    cost = dict(flops=1_100_000_000, bytes_accessed=5 << 20)

    dprev, a, second, keep2, send2 = call(
        two_kernel,
        [((users, FEAT), F32), ((OWNERS, 80, HALF), BF), ((OWNERS, 64, HALF), BF), ((FEAT, FEAT), F32), ((FEAT, FEAT), F32)],
        [SMEM] * 4 + [VMEM] * 7,
        scratch + [pltpu.SMEM((2 * OWNERS,), jnp.int32)],
        **cost,
    )(tile_user, counts, dest, item_block, cotangent, pre_two, message_two, pre_one, w_self, w_inter, adjacency)
    got_a = to_owners(a)

    user_grad, c, d_items, keep1, send1 = call(
        one_kernel,
        [((users, FEAT), BF), ((OWNERS, 96, HALF), BF), ((OWNERS, 32, HALF), BF), ((FEAT, FEAT), F32), ((FEAT, FEAT), F32)],
        [SMEM] * 3 + [VMEM] * 7,
        scratch,
        **cost,
    )(tile_user, counts, dest, dprev, pre_one, message_one, users_zero, w_self, w_inter, adjacency)
    got2 = lax.ppermute(send2, "rep", swap)
    got1 = lax.ppermute(send1, "rep", swap)
    (b,) = call(pack_kernel, [((OWNERS, 96, HALF), BF)], [VMEM] * 5, flops=1_000_000, bytes_accessed=2 << 20)(
        second, keep2, got2, keep1, got1
    )
    got_b = to_owners(b)

    (total,) = call(chunk_kernel, [((32, HALF), F32)], [VMEM], flops=1_000_000, bytes_accessed=1 << 18)(got_b)
    got_c = to_owners(c)
    total = total + lax.ppermute(total, "rep", along_z(lambda z: z ^ 1))
    total = total + lax.ppermute(total, "rep", along_z(lambda z: z ^ 2))
    z_chips = reps // 2
    total = (
        total
        + lax.ppermute(total, "rep", along_z(lambda z: (z + 4) % z_chips))
        + lax.ppermute(total, "rep", along_z(lambda z: (z + 8) % z_chips))
    )
    d = jnp.concatenate([d_items, jnp.broadcast_to(total.astype(BF)[None], (OWNERS, 32, HALF))], axis=1)
    got_d = to_owners(d)

    index = got_a[:, 64:80:8, 0].astype(jnp.int32).reshape(2 * OWNERS)
    acc = [pltpu.VMEM((TRASH + 1, 64, HALF), F32)]
    item = [((OWNERS * RB, FEAT), BF)]
    (item_one,) = call(
        functools.partial(collect_kernel, (((0, 0, 0, 64),), ((1, 0, 0, 64),))),
        item, [SMEM, VMEM, VMEM], acc, flops=1_000_000, bytes_accessed=3 << 20,
    )(index, got_a, got_b)
    other = lax.ppermute(got_d[:, 32:64], "rep", swap)
    (item_zero,) = call(
        functools.partial(collect_kernel, (((0, 0, 0, 64), (1, 64, 0, 32)), ((1, 0, 32, 32),))),
        item, [SMEM, VMEM, VMEM], acc, flops=1_000_000, bytes_accessed=3 << 20,
    )(index, got_c, got_d)
    self_grad, inter_grad = call(
        unpack_kernel, [((2, FEAT, FEAT), F32)] * 2, [VMEM] * 2, flops=1_000_000, bytes_accessed=2 << 20
    )(got_d, other)
    return user_grad, item_one, item_zero, self_grad, inter_grad


def solution(mesh):
    both = ("owner", "rep")
    rows = P(both, None)
    return jax.shard_map(
        local,
        mesh=mesh,
        in_specs=(rows,) * 6 + (P(), P(), P(both, None, None), P(both), P(both), rows, P(both)),
        out_specs=(rows, rows, rows, P(), P()),
        check_vma=False,
    )
```

```python
import functools

import jax
import jax.numpy as jnp
from jax import lax
from jax.experimental import pallas as pl
from jax.experimental.pallas import tpu as pltpu
from jax.sharding import PartitionSpec as P

BF = jnp.bfloat16
F32 = jnp.float32
SLOPE = 0.2
RB = 32
FEAT = 256
HALF = 128
BLK = 256
OWNERS = 32
TRASH = 32
VMEM = pl.BlockSpec(memory_space=pltpu.VMEM)
SMEM = pl.BlockSpec(memory_space=pltpu.SMEM)
HBM = pl.BlockSpec(memory_space=pltpu.HBM)
ANY = pl.BlockSpec(memory_space=pl.ANY)
PARAMS = pltpu.CompilerParams(vmem_limit_bytes=12 * 1024 * 1024)
WIDE = pltpu.CompilerParams(vmem_limit_bytes=60 * 1024 * 1024)


def tdot(a, b):
    return lax.dot_general(a, b, (((0,), (0,)), ((), ())), preferred_element_type=F32)


def dot_t(a, b):
    return lax.dot_general(a, b, (((1,), (1,)), ((), ())), preferred_element_type=F32)


def user_kernel(*refs):
    ins, rest = refs[:8], refs[8:]
    dmsg2_ref, dmsg1_ref, user_grad_ref, keep_ref, send_ref = rest[:5]
    bufs, sum2_s, prod2_s, delta2_s, sum1_s, prod1_s, delta1_s, sems = rest[5:13], *rest[13:]
    blocks = ins[0].shape[0] // BLK
    weights = [pltpu.make_async_copy(ins[i], bufs[i], sems.at[i]) for i in (6, 7)]
    for copy in weights:
        copy.start()
    loads = []
    for b in range(blocks):
        rows = pl.ds(b * BLK, BLK)
        loads.append(
            [pltpu.make_async_copy(ins[i].at[rows], bufs[i].at[rows], sems.at[8 + 6 * b + i]) for i in range(6)]
        )
        for copy in loads[-1]:
            copy.start()
    cot, pre2, pre1, msg2, msg1, zero, ws, wi = bufs
    for copy in weights:
        copy.wait()
    for b in range(blocks):
        rows = pl.ds(b * BLK, BLK)
        for copy in loads[b]:
            copy.wait()
        one = pre1[rows, :].astype(F32)
        prev = jnp.where(one > 0, one, SLOPE * one).astype(BF).astype(F32)
        deltas = (cot[rows, :].astype(F32) * jnp.where(pre2[rows, :].astype(F32) > 0, 1.0, SLOPE)).astype(BF)
        msg = msg2[rows, :].astype(F32)
        delta2_s[rows, :] = deltas
        sum2_s[rows, :] = (msg + prev).astype(BF)
        prod2_s[rows, :] = (msg * prev).astype(BF)
        back_self = dot_t(deltas, ws[1])
        back_inter = dot_t(deltas, wi[1])
        dmsg2_ref[rows, :] = (back_self + back_inter * prev).astype(BF)
        dprev = back_self + back_inter * msg
        deltas = (dprev * jnp.where(one > 0, 1.0, SLOPE)).astype(BF)
        msg = msg1[rows, :].astype(F32)
        prev = zero[rows, :].astype(F32)
        delta1_s[rows, :] = deltas
        sum1_s[rows, :] = (msg + prev).astype(BF)
        prod1_s[rows, :] = (msg * prev).astype(BF)
        back_self = dot_t(deltas, ws[0])
        back_inter = dot_t(deltas, wi[0])
        dmsg1_ref[rows, :] = (back_self + back_inter * prev).astype(BF)
        user_grad_ref[rows, :] = (back_self + back_inter * msg).astype(BF)
    even = lax.rem(lax.axis_index("rep"), 2) == 0
    for at, (sum_s, prod_s, delta_s) in enumerate(((sum2_s, prod2_s, delta2_s), (sum1_s, prod1_s, delta1_s))):
        grad_self = tdot(sum_s[...], delta_s[...])
        grad_inter = tdot(prod_s[...], delta_s[...])
        keep_ref[at] = jnp.where(even, grad_self, grad_inter)
        send_ref[at] = jnp.where(even, grad_inter, grad_self)


def rank_blocks(dest_ref, rank_s, seen_s):
    for o in range(OWNERS):
        seen_s[o] = 0
    for j in range(dest_ref.shape[0]):
        o = dest_ref[j]
        rank_s[j] = seen_s[o]
        seen_s[o] = seen_s[o] + 1


def tile_terms(user_ref, count_ref, dest_ref, adj_ref, dmsg_ref, rank_s, out_ref):
    for t in range(adj_ref.shape[0]):
        start = pl.multiple_of(user_ref[t] * BLK, BLK)
        part = tdot(adj_ref[t], dmsg_ref[pl.ds(start, BLK), :])
        live = lax.broadcasted_iota(jnp.int32, part.shape, 0) < count_ref[t]
        part = jnp.where(live, part, 0.0).astype(BF)
        for b in range(part.shape[0] // RB):
            j = t * (part.shape[0] // RB) + b
            at = pl.multiple_of(rank_s[j] * 64, 64)
            block = part[b * RB : (b + 1) * RB, :]
            out_ref[dest_ref[j], pl.ds(at, RB), :] = block[:, :HALF]
            out_ref[dest_ref[j], pl.ds(at + RB, RB), :] = block[:, HALF:]


def two_kernel(user_ref, count_ref, dest_ref, item_ref, adj_ref, dmsg_ref, a_ref, rank_s, seen_s, tab_s):
    rank_blocks(dest_ref, rank_s, seen_s)
    for i in range(2 * OWNERS):
        tab_s[i] = TRASH
    for j in range(dest_ref.shape[0]):
        tab_s[2 * dest_ref[j] + rank_s[j]] = item_ref[j]
    a_ref[...] = jnp.zeros_like(a_ref)
    top = lax.broadcasted_iota(jnp.int32, (16, HALF), 0) < 8
    for o in range(OWNERS):
        a_ref[o, 128:144, :] = jnp.where(top, tab_s[2 * o], tab_s[2 * o + 1]).astype(F32).astype(BF)
    tile_terms(user_ref, count_ref, dest_ref, adj_ref, dmsg_ref, rank_s, a_ref)


def one_kernel(user_ref, count_ref, dest_ref, adj_ref, dmsg_ref, b_ref, rank_s, seen_s):
    rank_blocks(dest_ref, rank_s, seen_s)
    b_ref[...] = jnp.zeros_like(b_ref)
    tile_terms(user_ref, count_ref, dest_ref, adj_ref, dmsg_ref, rank_s, b_ref)


def pack_kernel(keep_ref, got_ref, items_ref, a_ref, grads_s, sem):
    for o in range(OWNERS):
        rows = slice(8 * o, 8 * o + 8)
        for at in range(2):
            total = keep_ref[at, rows, :] + got_ref[at, rows, :]
            grads_s[o, 16 * at : 16 * at + 16, :] = jnp.concatenate([total[:, :HALF], total[:, HALF:]], axis=0).astype(BF)
    copy = pltpu.make_async_copy(grads_s, a_ref.at[:, pl.ds(144, 32), :], sem)
    copy.start()
    copy.wait()


def chunk_kernel(a_ref, total_ref):
    acc = a_ref[0, 144:176, :].astype(F32)
    for s in range(1, OWNERS):
        acc = acc + a_ref[s, 144:176, :].astype(F32)
    total_ref[...] = acc


def collect_kernel(index_ref, in_ref, out_ref, acc_s):
    acc_s[...] = jnp.zeros_like(acc_s)

    def body(s, carry):
        for slot in range(2):
            i = index_ref[2 * s + slot]
            acc_s[i] += in_ref[s, 64 * slot : 64 * slot + 64, :].astype(F32)
        return carry

    lax.fori_loop(0, OWNERS, body, 0, unroll=4)
    for i in range(TRASH):
        out_ref[RB * i : RB * i + RB, :HALF] = acc_s[i, 0:32, :].astype(BF)
        out_ref[RB * i : RB * i + RB, HALF:] = acc_s[i, 32:64, :].astype(BF)


def unpack_kernel(mine_ref, other_ref, self_ref, inter_ref):
    even = lax.rem(lax.axis_index("rep"), 2) == 0
    for o in range(OWNERS):
        mine = mine_ref[o].astype(F32)
        other = other_ref[o].astype(F32)
        a = jnp.where(even, mine, other)
        b = jnp.where(even, other, mine)
        rows = slice(8 * o, 8 * o + 8)
        for ref, value in ((self_ref, a), (inter_ref, b)):
            ref[1, rows, :HALF] = value[0:8]
            ref[1, rows, HALF:] = value[8:16]
            ref[0, rows, :HALF] = value[16:24]
            ref[0, rows, HALF:] = value[24:32]


def call(kernel, outs, in_specs, scratch=(), aliases=(), params=PARAMS, out_spec=VMEM, **cost):
    return pl.pallas_call(
        kernel,
        out_shape=[jax.ShapeDtypeStruct(s, d) for s, d in outs],
        in_specs=in_specs,
        out_specs=[out_spec] * len(outs),
        scratch_shapes=list(scratch),
        compiler_params=params,
        input_output_aliases=dict(aliases),
        cost_estimate=pl.CostEstimate(transcendentals=0, **cost),
    )


def local(cotangent, pre_two, pre_one, message_two, message_one, users_zero, w_self, w_inter, adjacency, tile_user,
          counts, dest, item_block):
    users = cotangent.shape[0]
    reps = lax.axis_size("rep")
    z_chips = reps // 2
    swap = [(i, i ^ 1) for i in range(reps)]
    dest = dest.reshape(dest.shape[0])

    def along_z(step):
        return [(2 * z + c, 2 * step(z) + c) for z in range(z_chips) for c in range(2)]

    def to_owners(x):
        return lax.all_to_all(x, "owner", split_axis=0, concat_axis=0, tiled=True)

    user = ((users, FEAT), BF)
    both = ((2, FEAT, FEAT), F32)
    ranks = [pltpu.SMEM((OWNERS,), jnp.int32)] * 2
    dmsg2, dmsg1, user_grad, keep, send = call(
        user_kernel,
        [user, user, user, both, both],
        [HBM] * 8,
        [pltpu.VMEM((users, FEAT), BF)] * 6 + [pltpu.VMEM((2, FEAT, FEAT), BF)] * 2
        + [pltpu.VMEM((users, FEAT), BF)] * 6 + [pltpu.SemaphoreType.DMA((8 + 6 * (users // BLK),))],
        params=WIDE, flops=900_000_000, bytes_accessed=6 << 20,
    )(cotangent, pre_two, pre_one, message_two, message_one, users_zero, w_self, w_inter)
    got = lax.ppermute(send, "rep", swap)
    (items,) = call(
        two_kernel, [((OWNERS, 176, HALF), BF)], [SMEM] * 4 + [VMEM] * 2,
        ranks + [pltpu.SMEM((2 * OWNERS,), jnp.int32)], flops=140_000_000, bytes_accessed=2 << 20,
    )(tile_user, counts, dest, item_block, adjacency, dmsg2)
    (a,) = call(
        pack_kernel, [((OWNERS, 176, HALF), BF)], [VMEM, VMEM, ANY],
        [pltpu.VMEM((OWNERS, 32, HALF), BF), pltpu.SemaphoreType.DMA], aliases={2: 0}, out_spec=ANY,
        flops=1_000_000, bytes_accessed=2 << 20,
    )(keep, got, items)
    got_a = to_owners(a)

    (b,) = call(
        one_kernel, [((OWNERS, 128, HALF), BF)], [SMEM] * 3 + [VMEM] * 2, ranks,
        flops=140_000_000, bytes_accessed=2 << 20,
    )(tile_user, counts, dest, adjacency, dmsg1)
    b, got_a = lax.optimization_barrier((b, got_a))
    got_b = to_owners(b)

    (total,) = call(chunk_kernel, [((32, HALF), F32)], [VMEM], flops=1_000_000, bytes_accessed=1 << 18)(got_a)
    total = total + lax.ppermute(total, "rep", along_z(lambda z: z ^ 1))
    total = total + lax.ppermute(total, "rep", along_z(lambda z: z ^ 2))
    total = (
        total
        + lax.ppermute(total, "rep", along_z(lambda z: (z + 4) % z_chips))
        + lax.ppermute(total, "rep", along_z(lambda z: (z + 8) % z_chips))
    )
    index = got_a[:, 128:144:8, 0].astype(jnp.int32).reshape(2 * OWNERS)
    acc = [pltpu.VMEM((TRASH + 1, 64, HALF), F32)]
    item = [((OWNERS * RB, FEAT), BF)]

    def collect(x):
        return call(collect_kernel, item, [SMEM, VMEM], acc, flops=1_000_000, bytes_accessed=3 << 20)(index, x)[0]

    item_one = collect(got_a)
    got_b, total = lax.optimization_barrier((got_b, total))
    mine = to_owners(jnp.broadcast_to(total.astype(BF)[None], (OWNERS, 32, HALF)))
    item_zero = collect(got_b)
    other = lax.ppermute(mine, "rep", swap)
    self_grad, inter_grad = call(
        unpack_kernel, [both] * 2, [VMEM] * 2, flops=1_000_000, bytes_accessed=2 << 20
    )(mine, other)
    return user_grad, item_one, item_zero, self_grad, inter_grad


def solution(mesh):
    both = ("owner", "rep")
    rows = P(both, None)
    return jax.shard_map(
        local,
        mesh=mesh,
        in_specs=(rows,) * 6 + (P(), P(), P(both, None, None), P(both), P(both), rows, P(both)),
        out_specs=(rows, rows, rows, P(), P()),
        check_vma=False,
    )
```

```python
import functools

import functools

import jax
import jax.numpy as jnp
from jax import lax
from jax.experimental import pallas as pl
from jax.experimental.pallas import tpu as pltpu
from jax.sharding import PartitionSpec as P

BF = jnp.bfloat16
F32 = jnp.float32
SLOPE = 0.2
RB = 32
FEAT = 256
HALF = 128
BLK = 256
OWNERS = 32
TRASH = 32
NEAR = 3
VMEM = pl.BlockSpec(memory_space=pltpu.VMEM)
SMEM = pl.BlockSpec(memory_space=pltpu.SMEM)
HBM = pl.BlockSpec(memory_space=pltpu.HBM)
ANY = pl.BlockSpec(memory_space=pl.ANY)
PARAMS = pltpu.CompilerParams(vmem_limit_bytes=12 * 1024 * 1024)
FIT = pltpu.CompilerParams(vmem_limit_bytes=58 * 1024 * 1024)
WIDE = pltpu.CompilerParams(vmem_limit_bytes=60 * 1024 * 1024)


def tdot(a, b):
    return lax.dot_general(a, b, (((0,), (0,)), ((), ())), preferred_element_type=F32)


def dot_t(a, b):
    return lax.dot_general(a, b, (((1,), (1,)), ((), ())), preferred_element_type=F32)


def user_kernel(*refs):
    ins, rest = refs[:8], refs[8:]
    dmsg2_ref, dmsg1_ref, user_grad_ref, keep_ref, send_ref = rest[:5]
    bufs, sum2_s, prod2_s, delta2_s, sum1_s, prod1_s, delta1_s, sems = rest[5:13], *rest[13:]
    blocks = ins[0].shape[0] // BLK
    weights = [pltpu.make_async_copy(ins[i], bufs[i], sems.at[i]) for i in (6, 7)]
    for copy in weights:
        copy.start()
    loads = []
    for b in range(blocks):
        rows = pl.ds(b * BLK, BLK)
        loads.append(
            [pltpu.make_async_copy(ins[i].at[rows], bufs[i].at[rows], sems.at[8 + 6 * b + i]) for i in range(6)]
        )
        for copy in loads[-1]:
            copy.start()
    cot, pre2, pre1, msg2, msg1, zero, ws, wi = bufs
    for copy in weights:
        copy.wait()
    for b in range(blocks):
        rows = pl.ds(b * BLK, BLK)
        for copy in loads[b]:
            copy.wait()
        one = pre1[rows, :].astype(F32)
        prev = jnp.where(one > 0, one, SLOPE * one).astype(BF).astype(F32)
        deltas = (cot[rows, :].astype(F32) * jnp.where(pre2[rows, :].astype(F32) > 0, 1.0, SLOPE)).astype(BF)
        msg = msg2[rows, :].astype(F32)
        delta2_s[rows, :] = deltas
        sum2_s[rows, :] = (msg + prev).astype(BF)
        prod2_s[rows, :] = (msg * prev).astype(BF)
        back_self = dot_t(deltas, ws[1])
        back_inter = dot_t(deltas, wi[1])
        dmsg2_ref[rows, :] = (back_self + back_inter * prev).astype(BF)
        dprev = back_self + back_inter * msg
        deltas = (dprev * jnp.where(one > 0, 1.0, SLOPE)).astype(BF)
        msg = msg1[rows, :].astype(F32)
        prev = zero[rows, :].astype(F32)
        delta1_s[rows, :] = deltas
        sum1_s[rows, :] = (msg + prev).astype(BF)
        prod1_s[rows, :] = (msg * prev).astype(BF)
        back_self = dot_t(deltas, ws[0])
        back_inter = dot_t(deltas, wi[0])
        dmsg1_ref[rows, :] = (back_self + back_inter * prev).astype(BF)
        user_grad_ref[rows, :] = (back_self + back_inter * msg).astype(BF)
    even = lax.rem(lax.axis_index("rep"), 2) == 0
    for at, (sum_s, prod_s, delta_s) in enumerate(((sum2_s, prod2_s, delta2_s), (sum1_s, prod1_s, delta1_s))):
        grad_self = tdot(sum_s[...], delta_s[...])
        grad_inter = tdot(prod_s[...], delta_s[...])
        keep_ref[at] = jnp.where(even, grad_self, grad_inter)
        send_ref[at] = jnp.where(even, grad_inter, grad_self)


def rank_blocks(dest_ref, rank_s, seen_s):
    for o in range(OWNERS):
        seen_s[o] = 0
    for j in range(dest_ref.shape[0]):
        o = dest_ref[j]
        rank_s[j] = seen_s[o]
        seen_s[o] = seen_s[o] + 1


def tile_terms(user_ref, count_ref, dest_ref, adj_ref, dmsg_ref, rank_s, store):
    for t in range(adj_ref.shape[0]):
        start = pl.multiple_of(user_ref[t] * BLK, BLK)
        part = tdot(adj_ref[t], dmsg_ref[pl.ds(start, BLK), :])
        live = lax.broadcasted_iota(jnp.int32, part.shape, 0) < count_ref[t]
        part = jnp.where(live, part, 0.0).astype(BF)
        for b in range(part.shape[0] // RB):
            j = t * (part.shape[0] // RB) + b
            store(dest_ref[j], rank_s[j], part[b * RB : (b + 1) * RB, :])


def two_kernel(user_ref, count_ref, dest_ref, item_ref, adj_hbm, dmsg_hbm, a_ref, b_ref, adj_s, dmsg_s, sems, rank_s,
               seen_s, tab_s):
    copies = [pltpu.make_async_copy(dmsg_hbm, dmsg_s, sems.at[0]), pltpu.make_async_copy(adj_hbm, adj_s, sems.at[1])]
    for copy in copies:
        copy.start()
    rank_blocks(dest_ref, rank_s, seen_s)
    for i in range(2 * OWNERS):
        tab_s[i] = TRASH
    for j in range(dest_ref.shape[0]):
        tab_s[2 * dest_ref[j] + rank_s[j]] = item_ref[j]
    a_ref[...] = jnp.zeros_like(a_ref)
    b_ref[...] = jnp.zeros_like(b_ref)
    top = lax.broadcasted_iota(jnp.int32, (16, HALF), 0) < 8
    for o in range(OWNERS):
        b_ref[o, 64:80, :] = jnp.where(top, tab_s[2 * o], tab_s[2 * o + 1]).astype(F32).astype(BF)
    for copy in copies:
        copy.wait()

    def store(o, rank, block):
        @pl.when(rank == 0)
        def _():
            a_ref[o, 0:32, :] = block[:, :HALF]
            a_ref[o, 32:64, :] = block[:, HALF:]

        @pl.when(rank != 0)
        def _():
            b_ref[o, 0:32, :] = block[:, :HALF]
            b_ref[o, 32:64, :] = block[:, HALF:]

    tile_terms(user_ref, count_ref, dest_ref, adj_s, dmsg_s, rank_s, store)


def one_kernel(user_ref, count_ref, dest_ref, adj_hbm, dmsg_hbm, items_ref, b_ref, c_ref, adj_s, dmsg_s, part_s, sems,
               rank_s, seen_s):
    copies = [pltpu.make_async_copy(dmsg_hbm, dmsg_s, sems.at[0]), pltpu.make_async_copy(adj_hbm, adj_s, sems.at[1])]
    for copy in copies:
        copy.start()
    rank_blocks(dest_ref, rank_s, seen_s)
    part_s[...] = jnp.zeros_like(part_s)
    c_ref[...] = jnp.zeros_like(c_ref)
    for copy in copies:
        copy.wait()

    def store(o, rank, block):
        @pl.when(rank == 0)
        def _():
            c_ref[o, 0:32, :] = block[:, :HALF]
            c_ref[o, 32:64, :] = block[:, HALF:]

        @pl.when(rank != 0)
        def _():
            c_ref[o, 64:96, :] = block[:, :HALF]
            part_s[o] = block[:, HALF:]

    tile_terms(user_ref, count_ref, dest_ref, adj_s, dmsg_s, rank_s, store)
    copy = pltpu.make_async_copy(part_s, b_ref.at[:, pl.ds(80, 32), :], sems.at[2])
    copy.start()
    copy.wait()


def pack_kernel(keep_hbm, got_hbm, items_ref, a_ref, keep_s, got_s, grads_s, sems):
    copies = [pltpu.make_async_copy(keep_hbm, keep_s, sems.at[0]), pltpu.make_async_copy(got_hbm, got_s, sems.at[1])]
    for copy in copies:
        copy.start()
    for copy in copies:
        copy.wait()
    for o in range(OWNERS):
        rows = slice(8 * o, 8 * o + 8)
        for at in range(2):
            total = keep_s[at, rows, :] + got_s[at, rows, :]
            grads_s[o, 16 * at : 16 * at + 16, :] = jnp.concatenate([total[:, :HALF], total[:, HALF:]], axis=0).astype(BF)
    copy = pltpu.make_async_copy(grads_s, a_ref.at[:, pl.ds(64, 32), :], sems.at[2])
    copy.start()
    copy.wait()


def chunk_kernel(a_ref, total_ref):
    acc = a_ref[0, 64:96, :].astype(F32)
    for s in range(1, OWNERS):
        acc = acc + a_ref[s, 64:96, :].astype(F32)
    total_ref[...] = acc


def ordered_sum(position, refs, slots_s):
    for k, ref in enumerate(refs):
        slots_s[lax.rem(position + len(refs) - k, len(refs))] = ref[...]
    total = slots_s[0]
    for k in range(1, len(refs)):
        total = total + slots_s[k]
    return total


def near_kernel(*refs):
    *ins, out_ref, slots_s = refs
    chip = lax.axis_index("rep") // 2
    out_ref[...] = ordered_sum(lax.rem(chip, NEAR), ins, slots_s)


def far_kernel(*refs):
    *ins, items_ref, c_ref, slots_s, copies_s, sem = refs
    chip = lax.axis_index("rep") // 2
    total = ordered_sum(chip // NEAR, ins, slots_s).astype(BF)
    for o in range(OWNERS):
        copies_s[o] = total
    copy = pltpu.make_async_copy(copies_s, c_ref.at[:, pl.ds(96, 32), :], sem)
    copy.start()
    copy.wait()


def collect_kernel(cuts, index_ref, *refs):
    *in_refs, out_ref, acc_s = refs
    acc_s[...] = jnp.zeros_like(acc_s)

    def body(s, carry):
        for ref, pieces in zip(in_refs, cuts):
            for slot, at, to, rows in pieces:
                i = index_ref[2 * s + slot]
                acc_s[i, to : to + rows, :] += ref[s, at : at + rows, :].astype(F32)
        return carry

    lax.fori_loop(0, OWNERS, body, 0, unroll=4)
    for i in range(TRASH):
        out_ref[RB * i : RB * i + RB, :HALF] = acc_s[i, 0:32, :].astype(BF)
        out_ref[RB * i : RB * i + RB, HALF:] = acc_s[i, 32:64, :].astype(BF)


def unpack_kernel(mine_ref, other_ref, self_ref, inter_ref):
    even = lax.rem(lax.axis_index("rep"), 2) == 0
    for o in range(OWNERS):
        mine = mine_ref[o, 96:128, :].astype(F32)
        other = other_ref[o].astype(F32)
        a = jnp.where(even, mine, other)
        b = jnp.where(even, other, mine)
        rows = slice(8 * o, 8 * o + 8)
        for ref, value in ((self_ref, a), (inter_ref, b)):
            ref[1, rows, :HALF] = value[0:8]
            ref[1, rows, HALF:] = value[8:16]
            ref[0, rows, :HALF] = value[16:24]
            ref[0, rows, HALF:] = value[24:32]


def call(kernel, outs, in_specs, scratch=(), aliases=(), params=PARAMS, out_specs=None, **cost):
    return pl.pallas_call(
        kernel,
        out_shape=[jax.ShapeDtypeStruct(s, d) for s, d in outs],
        in_specs=in_specs,
        out_specs=out_specs or [VMEM] * len(outs),
        scratch_shapes=list(scratch),
        compiler_params=params,
        input_output_aliases=dict(aliases),
        cost_estimate=pl.CostEstimate(transcendentals=0, **cost),
    )


def local(cotangent, pre_two, pre_one, message_two, message_one, users_zero, w_self, w_inter, adjacency, tile_user,
          counts, dest, item_block):
    users = cotangent.shape[0]
    reps = lax.axis_size("rep")
    z_chips = reps // 2
    swap = [(i, i ^ 1) for i in range(reps)]
    dest = dest.reshape(dest.shape[0])

    def from_z(x, before):
        return lax.ppermute(x, "rep", [(2 * before(z) + c, 2 * z + c) for z in range(z_chips) for c in range(2)])

    def to_owners(x):
        return lax.all_to_all(x, "owner", split_axis=0, concat_axis=0, tiled=True)

    user = ((users, FEAT), BF)
    both = ((2, FEAT, FEAT), F32)
    chunk = ((32, HALF), F32)
    tiles = [pltpu.VMEM(adjacency.shape, BF), pltpu.VMEM((users, FEAT), BF)]
    ranks = [pltpu.SMEM((OWNERS,), jnp.int32)] * 2
    small = dict(flops=1_000_000, bytes_accessed=2 << 20)
    dmsg2, dmsg1, user_grad, keep, send = call(
        user_kernel,
        [user, user, user, both, both],
        [HBM] * 8,
        [pltpu.VMEM((users, FEAT), BF)] * 6 + [pltpu.VMEM((2, FEAT, FEAT), BF)] * 2
        + [pltpu.VMEM((users, FEAT), BF)] * 6 + [pltpu.SemaphoreType.DMA((8 + 6 * (users // BLK),))],
        params=WIDE, flops=900_000_000, bytes_accessed=6 << 20,
    )(cotangent, pre_two, pre_one, message_two, message_one, users_zero, w_self, w_inter)
    got = lax.ppermute(send, "rep", swap)
    a_items, b_items = call(
        two_kernel, [((OWNERS, 96, HALF), BF), ((OWNERS, 112, HALF), BF)], [SMEM] * 4 + [HBM] * 2,
        tiles + [pltpu.SemaphoreType.DMA((2,))] + ranks + [pltpu.SMEM((2 * OWNERS,), jnp.int32)],
        params=WIDE, flops=140_000_000, bytes_accessed=2 << 20,
    )(tile_user, counts, dest, item_block, adjacency, dmsg2)
    (a,) = call(
        pack_kernel, [((OWNERS, 96, HALF), BF)], [HBM, HBM, ANY],
        [pltpu.VMEM(both[0], F32)] * 2 + [pltpu.VMEM((OWNERS, 32, HALF), BF), pltpu.SemaphoreType.DMA((3,))],
        aliases={2: 0}, out_specs=[ANY], params=FIT, **small,
    )(keep, got, a_items)
    got_a = to_owners(a)

    b, c_items = call(
        one_kernel, [((OWNERS, 112, HALF), BF), ((OWNERS, 128, HALF), BF)], [SMEM] * 3 + [HBM] * 2 + [ANY],
        tiles + [pltpu.VMEM((OWNERS, 32, HALF), BF), pltpu.SemaphoreType.DMA((3,))] + ranks,
        aliases={5: 0}, out_specs=[ANY, VMEM], params=WIDE, flops=140_000_000, bytes_accessed=2 << 20,
    )(tile_user, counts, dest, adjacency, dmsg1, b_items)
    b, got_a = lax.optimization_barrier((b, got_a))
    got_b = to_owners(b)

    (total,) = call(chunk_kernel, [chunk], [VMEM], **small)(got_a)
    near = [total] + [from_z(total, lambda z, k=k: z - z % NEAR + (z + NEAR - k) % NEAR) for k in range(1, NEAR)]
    (total,) = call(near_kernel, [chunk], [VMEM] * NEAR, [pltpu.VMEM((NEAR, 32, HALF), F32)], **small)(*near)
    groups = z_chips // NEAR
    far = [total] + [from_z(total, lambda z, k=k: (z + z_chips - NEAR * k) % z_chips) for k in range(1, groups)]
    (c,) = call(
        far_kernel, [((OWNERS, 128, HALF), BF)], [VMEM] * groups + [ANY],
        [pltpu.VMEM((groups, 32, HALF), F32), pltpu.VMEM((OWNERS, 32, HALF), BF), pltpu.SemaphoreType.DMA],
        aliases={groups: 0}, out_specs=[ANY], params=FIT, **small,
    )(*far, c_items)
    c, got_b = lax.optimization_barrier((c, got_b))
    got_c = to_owners(c)

    index = got_b[:, 64:80:8, 0].astype(jnp.int32).reshape(2 * OWNERS)

    def collect(cuts, *arrays):
        return call(
            functools.partial(collect_kernel, cuts), [((OWNERS * RB, FEAT), BF)], [SMEM] + [VMEM] * len(arrays),
            [pltpu.VMEM((TRASH + 1, 64, HALF), F32)], **small,
        )(index, *arrays)[0]

    item_one = collect((((0, 0, 0, 64),), ((1, 0, 0, 64),)), got_a, got_b)
    got_c, item_one = lax.optimization_barrier((got_c, item_one))
    other = lax.ppermute(got_c[:, 96:128], "rep", swap)
    item_zero = collect((((0, 0, 0, 64), (1, 64, 0, 32)), ((1, 80, 32, 32),)), got_c, got_b)
    self_grad, inter_grad = call(unpack_kernel, [both] * 2, [VMEM] * 2, **small)(got_c, other)
    return user_grad, item_one, item_zero, self_grad, inter_grad


def solution(mesh):
    both = ("owner", "rep")
    rows = P(both, None)
    return jax.shard_map(
        local,
        mesh=mesh,
        in_specs=(rows,) * 6 + (P(), P(), P(both, None, None), P(both), P(both), rows, P(both)),
        out_specs=(rows, rows, rows, P(), P()),
        check_vma=False,
    )
```

```python
import functools

import functools

import jax
import jax.numpy as jnp
from jax import lax
from jax.experimental import pallas as pl
from jax.experimental.pallas import tpu as pltpu
from jax.sharding import PartitionSpec as P

BF = jnp.bfloat16
F32 = jnp.float32
SLOPE = 0.2
RB = 32
FEAT = 256
HALF = 128
BLK = 256
OWNERS = 32
TRASH = 32
NEAR = 4
VMEM = pl.BlockSpec(memory_space=pltpu.VMEM)
SMEM = pl.BlockSpec(memory_space=pltpu.SMEM)
HBM = pl.BlockSpec(memory_space=pltpu.HBM)
PARAMS = pltpu.CompilerParams(vmem_limit_bytes=12 * 1024 * 1024)
WIDE = pltpu.CompilerParams(vmem_limit_bytes=60 * 1024 * 1024)


def tdot(a, b):
    return lax.dot_general(a, b, (((0,), (0,)), ((), ())), preferred_element_type=F32)


def dot_t(a, b):
    return lax.dot_general(a, b, (((1,), (1,)), ((), ())), preferred_element_type=F32)


def user_kernel(*refs):
    ins, rest = refs[:8], refs[8:]
    dmsg2_ref, dmsg1_ref, user_grad_ref, keep_ref, send_ref = rest[:5]
    bufs, sum2_s, prod2_s, delta2_s, sum1_s, prod1_s, delta1_s, sems = rest[5:13], *rest[13:]
    blocks = ins[0].shape[0] // BLK
    weights = [pltpu.make_async_copy(ins[i], bufs[i], sems.at[i]) for i in (6, 7)]
    for copy in weights:
        copy.start()
    loads = []
    for b in range(blocks):
        rows = pl.ds(b * BLK, BLK)
        loads.append(
            [pltpu.make_async_copy(ins[i].at[rows], bufs[i].at[rows], sems.at[8 + 6 * b + i]) for i in range(6)]
        )
        for copy in loads[-1]:
            copy.start()
    cot, pre2, pre1, msg2, msg1, zero, ws, wi = bufs
    for copy in weights:
        copy.wait()
    for b in range(blocks):
        rows = pl.ds(b * BLK, BLK)
        for copy in loads[b]:
            copy.wait()
        one = pre1[rows, :].astype(F32)
        prev = jnp.where(one > 0, one, SLOPE * one).astype(BF).astype(F32)
        deltas = (cot[rows, :].astype(F32) * jnp.where(pre2[rows, :].astype(F32) > 0, 1.0, SLOPE)).astype(BF)
        msg = msg2[rows, :].astype(F32)
        delta2_s[rows, :] = deltas
        sum2_s[rows, :] = (msg + prev).astype(BF)
        prod2_s[rows, :] = (msg * prev).astype(BF)
        back_self = dot_t(deltas, ws[1])
        back_inter = dot_t(deltas, wi[1])
        dmsg2_ref[rows, :] = (back_self + back_inter * prev).astype(BF)
        dprev = back_self + back_inter * msg
        deltas = (dprev * jnp.where(one > 0, 1.0, SLOPE)).astype(BF)
        msg = msg1[rows, :].astype(F32)
        prev = zero[rows, :].astype(F32)
        delta1_s[rows, :] = deltas
        sum1_s[rows, :] = (msg + prev).astype(BF)
        prod1_s[rows, :] = (msg * prev).astype(BF)
        back_self = dot_t(deltas, ws[0])
        back_inter = dot_t(deltas, wi[0])
        dmsg1_ref[rows, :] = (back_self + back_inter * prev).astype(BF)
        user_grad_ref[rows, :] = (back_self + back_inter * msg).astype(BF)
    even = lax.rem(lax.axis_index("rep"), 2) == 0
    for at, (sum_s, prod_s, delta_s) in enumerate(((sum2_s, prod2_s, delta2_s), (sum1_s, prod1_s, delta1_s))):
        grad_self = tdot(sum_s[...], delta_s[...])
        grad_inter = tdot(prod_s[...], delta_s[...])
        keep_ref[at] = jnp.where(even, grad_self, grad_inter)
        send_ref[at] = jnp.where(even, grad_inter, grad_self)


def rank_blocks(dest_ref, rank_s, seen_s):
    for o in range(OWNERS):
        seen_s[o] = 0
    for j in range(dest_ref.shape[0]):
        o = dest_ref[j]
        rank_s[j] = seen_s[o]
        seen_s[o] = seen_s[o] + 1


def tile_terms(user_ref, count_ref, dest_ref, adj_ref, dmsg_ref, rank_s, out_ref):
    for t in range(adj_ref.shape[0]):
        start = pl.multiple_of(user_ref[t] * BLK, BLK)
        part = tdot(adj_ref[t], dmsg_ref[pl.ds(start, BLK), :])
        live = lax.broadcasted_iota(jnp.int32, part.shape, 0) < count_ref[t]
        part = jnp.where(live, part, 0.0).astype(BF)
        for b in range(part.shape[0] // RB):
            j = t * (part.shape[0] // RB) + b
            block = part[b * RB : (b + 1) * RB, :]
            out_ref[rank_s[j], dest_ref[j], 0:32, :] = block[:, :HALF]
            out_ref[rank_s[j], dest_ref[j], 32:64, :] = block[:, HALF:]


def two_kernel(user_ref, count_ref, dest_ref, item_ref, adj_ref, dmsg_ref, slots_ref, index_ref, rank_s, seen_s, tab_s):
    rank_blocks(dest_ref, rank_s, seen_s)
    for i in range(2 * OWNERS):
        tab_s[i] = TRASH
    for j in range(dest_ref.shape[0]):
        tab_s[2 * dest_ref[j] + rank_s[j]] = item_ref[j]
    slots_ref[...] = jnp.zeros_like(slots_ref)
    top = lax.broadcasted_iota(jnp.int32, (16, HALF), 0) < 8
    for o in range(OWNERS):
        index_ref[o] = jnp.where(top, tab_s[2 * o], tab_s[2 * o + 1]).astype(F32).astype(BF)
    tile_terms(user_ref, count_ref, dest_ref, adj_ref, dmsg_ref, rank_s, slots_ref)


def one_kernel(user_ref, count_ref, dest_ref, adj_ref, dmsg_ref, two_ref, index_ref, b_ref, rest_ref, slots_s, rank_s,
               seen_s):
    rank_blocks(dest_ref, rank_s, seen_s)
    slots_s[...] = jnp.zeros_like(slots_s)
    tile_terms(user_ref, count_ref, dest_ref, adj_ref, dmsg_ref, rank_s, slots_s)
    for o in range(OWNERS):
        b_ref[o, 0:64, :] = two_ref[1, o]
        b_ref[o, 64:80, :] = index_ref[o]
        b_ref[o, 80:144, :] = slots_s[0, o]
        b_ref[o, 144:176, :] = slots_s[1, o, 0:32, :]
        rest_ref[o] = slots_s[1, o, 32:64, :]


def pack_kernel(two_ref, keep_hbm, got_ref, a_ref, keep_ref, sem):
    copy = pltpu.make_async_copy(keep_hbm, keep_ref, sem)
    copy.start()
    for o in range(OWNERS):
        a_ref[o, 0:64, :] = two_ref[0, o]
    copy.wait()
    for o in range(OWNERS):
        rows = slice(8 * o, 8 * o + 8)
        for at in range(2):
            total = keep_ref[at, rows, :] + got_ref[at, rows, :]
            first = 64 + 16 * at
            a_ref[o, first : first + 16, :] = jnp.concatenate([total[:, :HALF], total[:, HALF:]], axis=0).astype(BF)


def chunk_kernel(a_ref, total_ref):
    acc = a_ref[0, 64:96, :].astype(F32)
    for s in range(1, OWNERS):
        acc = acc + a_ref[s, 64:96, :].astype(F32)
    total_ref[...] = acc


def last_kernel(own_ref, one_ref, two_ref, rest_ref, c_ref, slots_s):
    group = lax.axis_index("rep") // (2 * NEAR)
    for k, ref in enumerate((own_ref, one_ref, two_ref)):
        slots_s[lax.rem(group + 3 - k, 3)] = ref[...]
    total = (slots_s[0] + slots_s[1] + slots_s[2]).astype(BF)
    for o in range(OWNERS):
        c_ref[o, 0:32, :] = rest_ref[o]
        c_ref[o, 32:64, :] = total


def collect_kernel(cuts, index_ref, *refs):
    *in_refs, out_ref, acc_s = refs
    acc_s[...] = jnp.zeros_like(acc_s)

    def body(s, carry):
        for ref, pieces in zip(in_refs, cuts):
            for slot, at, to, rows in pieces:
                i = index_ref[2 * s + slot]
                acc_s[i, to : to + rows, :] += ref[s, at : at + rows, :].astype(F32)
        return carry

    lax.fori_loop(0, OWNERS, body, 0, unroll=4)
    for i in range(TRASH):
        out_ref[RB * i : RB * i + RB, :HALF] = acc_s[i, 0:32, :].astype(BF)
        out_ref[RB * i : RB * i + RB, HALF:] = acc_s[i, 32:64, :].astype(BF)


def unpack_kernel(mine_ref, other_ref, self_ref, inter_ref):
    even = lax.rem(lax.axis_index("rep"), 2) == 0
    for o in range(OWNERS):
        mine = mine_ref[o, 32:64, :].astype(F32)
        other = other_ref[o].astype(F32)
        a = jnp.where(even, mine, other)
        b = jnp.where(even, other, mine)
        rows = slice(8 * o, 8 * o + 8)
        for ref, value in ((self_ref, a), (inter_ref, b)):
            ref[1, rows, :HALF] = value[0:8]
            ref[1, rows, HALF:] = value[8:16]
            ref[0, rows, :HALF] = value[16:24]
            ref[0, rows, HALF:] = value[24:32]


def call(kernel, outs, in_specs, scratch=(), params=PARAMS, **cost):
    return pl.pallas_call(
        kernel,
        out_shape=[jax.ShapeDtypeStruct(s, d) for s, d in outs],
        in_specs=in_specs,
        out_specs=[VMEM] * len(outs),
        scratch_shapes=list(scratch),
        compiler_params=params,
        cost_estimate=pl.CostEstimate(transcendentals=0, **cost),
    )


def local(cotangent, pre_two, pre_one, message_two, message_one, users_zero, w_self, w_inter, adjacency, tile_user,
          counts, dest, item_block):
    users = cotangent.shape[0]
    reps = lax.axis_size("rep")
    z_chips = reps // 2
    swap = [(i, i ^ 1) for i in range(reps)]
    dest = dest.reshape(dest.shape[0])

    def from_z(x, source):
        return lax.ppermute(x, "rep", [(2 * source(z) + c, 2 * z + c) for z in range(z_chips) for c in range(2)])

    def to_owners(x):
        return lax.all_to_all(x, "owner", split_axis=0, concat_axis=0, tiled=True)

    def rows(n):
        return ((OWNERS, n, HALF), BF)

    user = ((users, FEAT), BF)
    both = ((2, FEAT, FEAT), F32)
    chunk = ((32, HALF), F32)
    ranks = [pltpu.SMEM((OWNERS,), jnp.int32)] * 2
    small = dict(flops=1_000_000, bytes_accessed=2 << 20)
    tile = dict(flops=140_000_000, bytes_accessed=2 << 20)
    dmsg2, dmsg1, user_grad, keep, send = call(
        user_kernel,
        [user, user, user, both, both],
        [HBM] * 8,
        [pltpu.VMEM((users, FEAT), BF)] * 6 + [pltpu.VMEM((2, FEAT, FEAT), BF)] * 2
        + [pltpu.VMEM((users, FEAT), BF)] * 6 + [pltpu.SemaphoreType.DMA((8 + 6 * (users // BLK),))],
        params=WIDE, flops=900_000_000, bytes_accessed=6 << 20,
    )(cotangent, pre_two, pre_one, message_two, message_one, users_zero, w_self, w_inter)
    got = lax.ppermute(send, "rep", swap)
    two, index_rows = call(
        two_kernel, [((2, OWNERS, 64, HALF), BF), rows(16)], [SMEM] * 4 + [VMEM] * 2,
        ranks + [pltpu.SMEM((2 * OWNERS,), jnp.int32)], **tile,
    )(tile_user, counts, dest, item_block, adjacency, dmsg2)
    (a,) = call(
        pack_kernel, [rows(96)], [VMEM, HBM, VMEM], [pltpu.VMEM(both[0], F32), pltpu.SemaphoreType.DMA], **small
    )(two, keep, got)
    got_a = to_owners(a)

    b, rest = call(
        one_kernel, [rows(176), rows(32)], [SMEM] * 3 + [VMEM] * 4,
        [pltpu.VMEM((2, OWNERS, 64, HALF), BF)] + ranks, **tile,
    )(tile_user, counts, dest, adjacency, dmsg1, two, index_rows)
    b, got_a = lax.optimization_barrier((b, got_a))
    got_b = to_owners(b)

    (total,) = call(chunk_kernel, [chunk], [VMEM], **small)(got_a)
    total = total + from_z(total, lambda z: z ^ 1)
    total = total + from_z(total, lambda z: z ^ 2)
    far = [from_z(total, lambda z, k=k: (z + z_chips - NEAR * k) % z_chips) for k in (1, 2)]
    (c,) = call(last_kernel, [rows(64)], [VMEM] * 4, [pltpu.VMEM((3, 32, HALF), F32)], **small)(total, *far, rest)
    c, got_b = lax.optimization_barrier((c, got_b))
    got_c = to_owners(c)

    index = got_b[:, 64:80:8, 0].astype(jnp.int32).reshape(2 * OWNERS)

    def collect(cuts, *arrays):
        return call(
            functools.partial(collect_kernel, cuts), [((OWNERS * RB, FEAT), BF)], [SMEM] + [VMEM] * len(arrays),
            [pltpu.VMEM((TRASH + 1, 64, HALF), F32)], **small,
        )(index, *arrays)[0]

    item_one = collect((((0, 0, 0, 64),), ((1, 0, 0, 64),)), got_a, got_b)
    got_c, item_one = lax.optimization_barrier((got_c, item_one))
    other = lax.ppermute(got_c[:, 32:64], "rep", swap)
    item_zero = collect((((0, 80, 0, 64), (1, 144, 0, 32)), ((1, 0, 32, 32),)), got_b, got_c)
    self_grad, inter_grad = call(unpack_kernel, [both] * 2, [VMEM] * 2, **small)(got_c, other)
    return user_grad, item_one, item_zero, self_grad, inter_grad


def solution(mesh):
    both = ("owner", "rep")
    rows = P(both, None)
    return jax.shard_map(
        local,
        mesh=mesh,
        in_specs=(rows,) * 6 + (P(), P(), P(both, None, None), P(both), P(both), rows, P(both)),
        out_specs=(rows, rows, rows, P(), P()),
        check_vma=False,
    )
```

```python
import functools

import functools

import jax
import jax.numpy as jnp
from jax import lax
from jax.experimental import pallas as pl
from jax.experimental.pallas import tpu as pltpu
from jax.sharding import PartitionSpec as P

BF = jnp.bfloat16
F32 = jnp.float32
SLOPE = 0.2
RB = 32
FEAT = 256
HALF = 128
BLK = 256
OWNERS = 32
XS = 4
YS = 8
INDEX = 128 * XS
ONES = INDEX + 16 * XS
TRASH = 32
NEAR = 4
VMEM = pl.BlockSpec(memory_space=pltpu.VMEM)
SMEM = pl.BlockSpec(memory_space=pltpu.SMEM)
HBM = pl.BlockSpec(memory_space=pltpu.HBM)
PARAMS = pltpu.CompilerParams(vmem_limit_bytes=12 * 1024 * 1024)
WIDE = pltpu.CompilerParams(vmem_limit_bytes=60 * 1024 * 1024)


def tdot(a, b):
    return lax.dot_general(a, b, (((0,), (0,)), ((), ())), preferred_element_type=F32)


def dot_t(a, b):
    return lax.dot_general(a, b, (((1,), (1,)), ((), ())), preferred_element_type=F32)


def user_kernel(*refs):
    ins, rest = refs[:8], refs[8:]
    dmsg2_ref, dmsg1_ref, user_grad_ref, keep_ref, send_ref = rest[:5]
    bufs, sum2_s, prod2_s, delta2_s, sum1_s, prod1_s, delta1_s, sems = rest[5:13], *rest[13:]
    blocks = ins[0].shape[0] // BLK
    weights = [pltpu.make_async_copy(ins[i], bufs[i], sems.at[i]) for i in (6, 7)]
    for copy in weights:
        copy.start()
    loads = []
    for b in range(blocks):
        rows = pl.ds(b * BLK, BLK)
        loads.append(
            [pltpu.make_async_copy(ins[i].at[rows], bufs[i].at[rows], sems.at[8 + 6 * b + i]) for i in range(6)]
        )
        for copy in loads[-1]:
            copy.start()
    cot, pre2, pre1, msg2, msg1, zero, ws, wi = bufs
    for copy in weights:
        copy.wait()
    for b in range(blocks):
        rows = pl.ds(b * BLK, BLK)
        for copy in loads[b]:
            copy.wait()
        one = pre1[rows, :].astype(F32)
        prev = jnp.where(one > 0, one, SLOPE * one).astype(BF).astype(F32)
        deltas = (cot[rows, :].astype(F32) * jnp.where(pre2[rows, :].astype(F32) > 0, 1.0, SLOPE)).astype(BF)
        msg = msg2[rows, :].astype(F32)
        delta2_s[rows, :] = deltas
        sum2_s[rows, :] = (msg + prev).astype(BF)
        prod2_s[rows, :] = (msg * prev).astype(BF)
        back_self = dot_t(deltas, ws[1])
        back_inter = dot_t(deltas, wi[1])
        dmsg2_ref[rows, :] = (back_self + back_inter * prev).astype(BF)
        dprev = back_self + back_inter * msg
        deltas = (dprev * jnp.where(one > 0, 1.0, SLOPE)).astype(BF)
        msg = msg1[rows, :].astype(F32)
        prev = zero[rows, :].astype(F32)
        delta1_s[rows, :] = deltas
        sum1_s[rows, :] = (msg + prev).astype(BF)
        prod1_s[rows, :] = (msg * prev).astype(BF)
        back_self = dot_t(deltas, ws[0])
        back_inter = dot_t(deltas, wi[0])
        dmsg1_ref[rows, :] = (back_self + back_inter * prev).astype(BF)
        user_grad_ref[rows, :] = (back_self + back_inter * msg).astype(BF)
    even = lax.rem(lax.axis_index("rep"), 2) == 0
    for at, (sum_s, prod_s, delta_s) in enumerate(((sum2_s, prod2_s, delta2_s), (sum1_s, prod1_s, delta1_s))):
        grad_self = tdot(sum_s[...], delta_s[...])
        grad_inter = tdot(prod_s[...], delta_s[...])
        keep_ref[at] = jnp.where(even, grad_self, grad_inter)
        send_ref[at] = jnp.where(even, grad_inter, grad_self)


def place_blocks(dest_ref, rank_s, place_s, seen_s):
    here = lax.rem(lax.axis_index("owner"), XS)
    for o in range(OWNERS):
        seen_s[o] = 0
    for j in range(dest_ref.shape[0]):
        o = dest_ref[j]
        rank_s[j] = seen_s[o]
        seen_s[o] = seen_s[o] + 1
        place_s[j] = lax.rem(lax.rem(o, XS) + XS - here, XS) * YS + o // XS


def tile_terms(user_ref, count_ref, adj_ref, dmsg_ref, rank_s, place_s, out_ref):
    for t in range(adj_ref.shape[0]):
        start = pl.multiple_of(user_ref[t] * BLK, BLK)
        part = tdot(adj_ref[t], dmsg_ref[pl.ds(start, BLK), :])
        live = lax.broadcasted_iota(jnp.int32, part.shape, 0) < count_ref[t]
        part = jnp.where(live, part, 0.0).astype(BF)
        for b in range(part.shape[0] // RB):
            j = t * (part.shape[0] // RB) + b
            block = part[b * RB : (b + 1) * RB, :]
            out_ref[rank_s[j], place_s[j], 0:32, :] = block[:, :HALF]
            out_ref[rank_s[j], place_s[j], 32:64, :] = block[:, HALF:]


def two_kernel(user_ref, count_ref, dest_ref, item_ref, adj_ref, dmsg_ref, *refs):
    *out_refs, slots_s, rank_s, place_s, seen_s, tab_s = refs
    place_blocks(dest_ref, rank_s, place_s, seen_s)
    for i in range(2 * OWNERS):
        tab_s[i] = TRASH
    for j in range(dest_ref.shape[0]):
        tab_s[2 * place_s[j] + rank_s[j]] = item_ref[j]
    slots_s[...] = jnp.zeros_like(slots_s)
    tile_terms(user_ref, count_ref, adj_ref, dmsg_ref, rank_s, place_s, slots_s)
    top = lax.broadcasted_iota(jnp.int32, (16, HALF), 0) < 8
    for k, out_ref in enumerate(out_refs):
        for y in range(YS):
            p = k * YS + y
            out_ref[y, 0:64, :] = slots_s[0, p]
            out_ref[y, 64:128, :] = slots_s[1, p]
            out_ref[y, 128:144, :] = jnp.where(top, tab_s[2 * p], tab_s[2 * p + 1]).astype(F32).astype(BF)


def one_kernel(user_ref, count_ref, dest_ref, adj_ref, dmsg_ref, out_ref, slots_s, rank_s, place_s, seen_s):
    place_blocks(dest_ref, rank_s, place_s, seen_s)
    slots_s[...] = jnp.zeros_like(slots_s)
    tile_terms(user_ref, count_ref, adj_ref, dmsg_ref, rank_s, place_s, slots_s)
    for k in range(XS):
        for y in range(YS):
            out_ref[y, 128 * k : 128 * k + 64, :] = slots_s[0, k * YS + y]
            out_ref[y, 128 * k + 64 : 128 * k + 128, :] = slots_s[1, k * YS + y]


def join_kernel(*refs):
    *two_refs, one_ref, out_ref = refs
    for y in range(YS):
        for k, ref in enumerate(two_refs):
            out_ref[y, 128 * k : 128 * k + 128, :] = ref[y, 0:128, :]
            out_ref[y, INDEX + 16 * k : INDEX + 16 * k + 16, :] = ref[y, 128:144, :]
        out_ref[y, ONES:, :] = one_ref[y]


def split_kernel(in_ref, *out_refs):
    for y in range(YS):
        for k, ref in enumerate(out_refs):
            at = ONES + 128 * (k + 1)
            ref[y] = in_ref[y, at : at + 128, :]


def pack_kernel(keep_ref, got_ref, a_ref):
    for o in range(OWNERS):
        rows = slice(8 * o, 8 * o + 8)
        for at in range(2):
            total = keep_ref[at, rows, :] + got_ref[at, rows, :]
            a_ref[o, 16 * at : 16 * at + 16, :] = jnp.concatenate([total[:, :HALF], total[:, HALF:]], axis=0).astype(BF)


def chunk_kernel(a_ref, total_ref):
    acc = a_ref[0].astype(F32)
    for s in range(1, OWNERS):
        acc = acc + a_ref[s].astype(F32)
    total_ref[...] = acc


def last_kernel(own_ref, one_ref, two_ref, c_ref, slots_s):
    group = lax.axis_index("rep") // (2 * NEAR)
    for k, ref in enumerate((own_ref, one_ref, two_ref)):
        slots_s[lax.rem(group + 3 - k, 3)] = ref[...]
    total = (slots_s[0] + slots_s[1] + slots_s[2]).astype(BF)
    for o in range(OWNERS):
        c_ref[o] = total


def collect_kernel(cuts, index_ref, *refs):
    *in_refs, out_ref, acc_s = refs
    acc_s[...] = jnp.zeros_like(acc_s)

    def body(y, carry):
        for ref, pieces in zip(in_refs, cuts):
            for k, at in pieces:
                for slot in range(2):
                    i = index_ref[2 * (XS * y + k) + slot]
                    acc_s[i] += ref[y, at + 64 * slot : at + 64 * slot + 64, :].astype(F32)
        return carry

    lax.fori_loop(0, YS, body, 0)
    for i in range(TRASH):
        out_ref[RB * i : RB * i + RB, :HALF] = acc_s[i, 0:32, :].astype(BF)
        out_ref[RB * i : RB * i + RB, HALF:] = acc_s[i, 32:64, :].astype(BF)


def unpack_kernel(mine_ref, other_ref, self_ref, inter_ref):
    even = lax.rem(lax.axis_index("rep"), 2) == 0
    for o in range(OWNERS):
        mine = mine_ref[o].astype(F32)
        other = other_ref[o].astype(F32)
        a = jnp.where(even, mine, other)
        b = jnp.where(even, other, mine)
        rows = slice(8 * o, 8 * o + 8)
        for ref, value in ((self_ref, a), (inter_ref, b)):
            ref[1, rows, :HALF] = value[0:8]
            ref[1, rows, HALF:] = value[8:16]
            ref[0, rows, :HALF] = value[16:24]
            ref[0, rows, HALF:] = value[24:32]


def call(kernel, outs, in_specs, scratch=(), params=PARAMS, **cost):
    return pl.pallas_call(
        kernel,
        out_shape=[jax.ShapeDtypeStruct(s, d) for s, d in outs],
        in_specs=in_specs,
        out_specs=[VMEM] * len(outs),
        scratch_shapes=list(scratch),
        compiler_params=params,
        cost_estimate=pl.CostEstimate(transcendentals=0, **cost),
    )


def local(cotangent, pre_two, pre_one, message_two, message_one, users_zero, w_self, w_inter, adjacency, tile_user,
          counts, dest, item_block):
    users = cotangent.shape[0]
    reps = lax.axis_size("rep")
    z_chips = reps // 2
    swap = [(i, i ^ 1) for i in range(reps)]
    dest = dest.reshape(dest.shape[0])

    def from_z(x, source):
        return lax.ppermute(x, "rep", [(2 * source(z) + c, 2 * z + c) for z in range(z_chips) for c in range(2)])

    def to_owners(x):
        return lax.all_to_all(x, "owner", split_axis=0, concat_axis=0, tiled=True)

    def along_x(x, k):
        return lax.ppermute(x, "owner", [(o, o - o % XS + (o + k) % XS) for o in range(OWNERS)])

    def rows(n, lead=OWNERS):
        return ((lead, n, HALF), BF)

    user = ((users, FEAT), BF)
    both = ((2, FEAT, FEAT), F32)
    chunk = ((32, HALF), F32)
    slots = [pltpu.VMEM((2, OWNERS, 64, HALF), BF)] + [pltpu.SMEM((OWNERS,), jnp.int32)] * 3
    small = dict(flops=1_000_000, bytes_accessed=2 << 20)
    tile = dict(flops=140_000_000, bytes_accessed=2 << 20)
    dmsg2, dmsg1, user_grad, keep, send = call(
        user_kernel,
        [user, user, user, both, both],
        [HBM] * 8,
        [pltpu.VMEM((users, FEAT), BF)] * 6 + [pltpu.VMEM((2, FEAT, FEAT), BF)] * 2
        + [pltpu.VMEM((users, FEAT), BF)] * 6 + [pltpu.SemaphoreType.DMA((8 + 6 * (users // BLK),))],
        params=WIDE, flops=900_000_000, bytes_accessed=6 << 20,
    )(cotangent, pre_two, pre_one, message_two, message_one, users_zero, w_self, w_inter)
    got = lax.ppermute(send, "rep", swap)
    two = call(
        two_kernel, [rows(144, YS)] * XS, [SMEM] * 4 + [VMEM] * 2, slots + [pltpu.SMEM((2 * OWNERS,), jnp.int32)], **tile
    )(tile_user, counts, dest, item_block, adjacency, dmsg2)
    keep, *two = lax.optimization_barrier((keep, *two))
    (a,) = call(pack_kernel, [rows(32)], [VMEM] * 2, **small)(keep, got)
    got_a = to_owners(a)

    two = [two[0]] + [along_x(two[k], k) for k in range(1, XS)]
    (one,) = call(one_kernel, [rows(128 * XS, YS)], [SMEM] * 3 + [VMEM] * 2, slots, **tile)(
        tile_user, counts, dest, adjacency, dmsg1
    )
    (b,) = call(join_kernel, [rows(272 * XS, YS)], [VMEM] * 5, **small)(*two, one)
    b, got_a = lax.optimization_barrier((b, got_a))
    got_b = lax.all_to_all(
        b, "owner", split_axis=0, concat_axis=0, tiled=True,
        axis_index_groups=[[XS * y + x for y in range(YS)] for x in range(XS)],
    )

    (total,) = call(chunk_kernel, [chunk], [VMEM], **small)(got_a)
    total = total + from_z(total, lambda z: z ^ 1)
    total = total + from_z(total, lambda z: z ^ 2)
    far = [from_z(total, lambda z, k=k: (z + z_chips - NEAR * k) % z_chips) for k in (1, 2)]
    (c,) = call(last_kernel, [rows(32)], [VMEM] * 3, [pltpu.VMEM((3, 32, HALF), F32)], **small)(total, *far)
    c, got_b = lax.optimization_barrier((c, got_b))
    got_c = to_owners(c)

    index = got_b[:, INDEX:ONES:8, 0].astype(jnp.int32).reshape(2 * OWNERS)

    def collect(cuts, *arrays):
        return call(
            functools.partial(collect_kernel, cuts), [((OWNERS * RB, FEAT), BF)], [SMEM] + [VMEM] * len(arrays),
            [pltpu.VMEM((TRASH + 1, 64, HALF), F32)], **small,
        )(index, *arrays)[0]

    ones = call(split_kernel, [rows(128, YS)] * (XS - 1), [VMEM], **small)(got_b)
    ones = [along_x(ones[k - 1], k) for k in range(1, XS)]
    item_one = collect((tuple((k, 128 * k) for k in range(XS)),), got_b)
    item_zero = collect((((0, ONES),),) + tuple(((k, 0),) for k in range(1, XS)), got_b, *ones)
    got_c, item_one, item_zero = lax.optimization_barrier((got_c, item_one, item_zero))
    other = lax.ppermute(got_c, "rep", swap)
    self_grad, inter_grad = call(unpack_kernel, [both] * 2, [VMEM] * 2, **small)(got_c, other)
    return user_grad, item_one, item_zero, self_grad, inter_grad


def solution(mesh):
    both = ("owner", "rep")
    rows = P(both, None)
    return jax.shard_map(
        local,
        mesh=mesh,
        in_specs=(rows,) * 6 + (P(), P(), P(both, None, None), P(both), P(both), rows, P(both)),
        out_specs=(rows, rows, rows, P(), P()),
        check_vma=False,
    )
```

```python
import functools

import functools

import jax
import jax.numpy as jnp
from jax import lax
from jax.experimental import pallas as pl
from jax.experimental.pallas import tpu as pltpu
from jax.sharding import PartitionSpec as P

BF = jnp.bfloat16
F32 = jnp.float32
SLOPE = 0.2
RB = 32
FEAT = 256
HALF = 128
BLK = 256
OWNERS = 32
TRASH = 32
NEAR = 4
VMEM = pl.BlockSpec(memory_space=pltpu.VMEM)
SMEM = pl.BlockSpec(memory_space=pltpu.SMEM)
HBM = pl.BlockSpec(memory_space=pltpu.HBM)
PARAMS = pltpu.CompilerParams(vmem_limit_bytes=12 * 1024 * 1024)
WIDE = pltpu.CompilerParams(vmem_limit_bytes=60 * 1024 * 1024)


def tdot(a, b):
    return lax.dot_general(a, b, (((0,), (0,)), ((), ())), preferred_element_type=F32)


def dot_t(a, b):
    return lax.dot_general(a, b, (((1,), (1,)), ((), ())), preferred_element_type=F32)


def user_kernel(*refs):
    ins, rest = refs[:8], refs[8:]
    dmsg2_ref, dmsg1_ref, user_grad_ref, keep_ref, send_ref = rest[:5]
    bufs, sum2_s, prod2_s, delta2_s, sum1_s, prod1_s, delta1_s, sems = rest[5:13], *rest[13:]
    blocks = ins[0].shape[0] // BLK
    weights = [pltpu.make_async_copy(ins[i], bufs[i], sems.at[i]) for i in (6, 7)]
    for copy in weights:
        copy.start()
    loads = []
    for b in range(blocks):
        rows = pl.ds(b * BLK, BLK)
        loads.append(
            [pltpu.make_async_copy(ins[i].at[rows], bufs[i].at[rows], sems.at[8 + 6 * b + i]) for i in range(6)]
        )
        for copy in loads[-1]:
            copy.start()
    cot, pre2, pre1, msg2, msg1, zero, ws, wi = bufs
    for copy in weights:
        copy.wait()
    for b in range(blocks):
        rows = pl.ds(b * BLK, BLK)
        for copy in loads[b]:
            copy.wait()
        one = pre1[rows, :].astype(F32)
        prev = jnp.where(one > 0, one, SLOPE * one).astype(BF).astype(F32)
        deltas = (cot[rows, :].astype(F32) * jnp.where(pre2[rows, :].astype(F32) > 0, 1.0, SLOPE)).astype(BF)
        msg = msg2[rows, :].astype(F32)
        delta2_s[rows, :] = deltas
        sum2_s[rows, :] = (msg + prev).astype(BF)
        prod2_s[rows, :] = (msg * prev).astype(BF)
        back_self = dot_t(deltas, ws[1])
        back_inter = dot_t(deltas, wi[1])
        dmsg2_ref[rows, :] = (back_self + back_inter * prev).astype(BF)
        dprev = back_self + back_inter * msg
        deltas = (dprev * jnp.where(one > 0, 1.0, SLOPE)).astype(BF)
        msg = msg1[rows, :].astype(F32)
        prev = zero[rows, :].astype(F32)
        delta1_s[rows, :] = deltas
        sum1_s[rows, :] = (msg + prev).astype(BF)
        prod1_s[rows, :] = (msg * prev).astype(BF)
        back_self = dot_t(deltas, ws[0])
        back_inter = dot_t(deltas, wi[0])
        dmsg1_ref[rows, :] = (back_self + back_inter * prev).astype(BF)
        user_grad_ref[rows, :] = (back_self + back_inter * msg).astype(BF)
    even = lax.rem(lax.axis_index("rep"), 2) == 0
    for at, (sum_s, prod_s, delta_s) in enumerate(((sum2_s, prod2_s, delta2_s), (sum1_s, prod1_s, delta1_s))):
        grad_self = tdot(sum_s[...], delta_s[...])
        grad_inter = tdot(prod_s[...], delta_s[...])
        keep_ref[at] = jnp.where(even, grad_self, grad_inter)
        send_ref[at] = jnp.where(even, grad_inter, grad_self).astype(BF)


def rank_blocks(dest_ref, rank_s, seen_s):
    for o in range(OWNERS):
        seen_s[o] = 0
    for j in range(dest_ref.shape[0]):
        o = dest_ref[j]
        rank_s[j] = seen_s[o]
        seen_s[o] = seen_s[o] + 1


def tile_terms(user_ref, count_ref, dest_ref, adj_ref, dmsg_ref, rank_s, out_ref):
    for t in range(adj_ref.shape[0]):
        start = pl.multiple_of(user_ref[t] * BLK, BLK)
        part = tdot(adj_ref[t], dmsg_ref[pl.ds(start, BLK), :])
        live = lax.broadcasted_iota(jnp.int32, part.shape, 0) < count_ref[t]
        part = jnp.where(live, part, 0.0).astype(BF)
        for b in range(part.shape[0] // RB):
            j = t * (part.shape[0] // RB) + b
            block = part[b * RB : (b + 1) * RB, :]
            out_ref[rank_s[j], dest_ref[j], 0:32, :] = block[:, :HALF]
            out_ref[rank_s[j], dest_ref[j], 32:64, :] = block[:, HALF:]


def two_kernel(user_ref, count_ref, dest_ref, item_ref, adj_ref, dmsg_ref, slots_ref, index_ref, rank_s, seen_s, tab_s):
    rank_blocks(dest_ref, rank_s, seen_s)
    for i in range(2 * OWNERS):
        tab_s[i] = TRASH
    for j in range(dest_ref.shape[0]):
        tab_s[2 * dest_ref[j] + rank_s[j]] = item_ref[j]
    slots_ref[...] = jnp.zeros_like(slots_ref)
    top = lax.broadcasted_iota(jnp.int32, (8, HALF), 0) < 4
    for o in range(OWNERS):
        index_ref[o] = jnp.where(top, tab_s[2 * o], tab_s[2 * o + 1]).astype(F32).astype(BF)
    tile_terms(user_ref, count_ref, dest_ref, adj_ref, dmsg_ref, rank_s, slots_ref)


def one_kernel(user_ref, count_ref, dest_ref, adj_ref, dmsg_ref, two_ref, index_ref, b_ref, rest_ref, slots_s, rank_s,
               seen_s):
    rank_blocks(dest_ref, rank_s, seen_s)
    slots_s[...] = jnp.zeros_like(slots_s)
    tile_terms(user_ref, count_ref, dest_ref, adj_ref, dmsg_ref, rank_s, slots_s)
    for o in range(OWNERS):
        b_ref[o, 0:32, :] = two_ref[0, o, 32:64, :]
        b_ref[o, 32:96, :] = two_ref[1, o]
        b_ref[o, 96:160, :] = slots_s[0, o]
        b_ref[o, 160:192, :] = slots_s[1, o, 0:32, :]
        b_ref[o, 192:200, :] = index_ref[o]
        rest_ref[o] = slots_s[1, o, 32:64, :]


def pack_kernel(two_ref, keep_ref, got_ref, a_ref):
    for o in range(OWNERS):
        a_ref[o, 0:32, :] = two_ref[0, o, 0:32, :]
        rows = slice(8 * o, 8 * o + 8)
        for at in range(2):
            total = keep_ref[at, rows, :] + got_ref[at, rows, :].astype(F32)
            first = 32 + 16 * at
            a_ref[o, first : first + 16, :] = jnp.concatenate([total[:, :HALF], total[:, HALF:]], axis=0).astype(BF)


def chunk_kernel(a_ref, total_ref):
    acc = a_ref[0, 32:64, :].astype(F32)
    for s in range(1, OWNERS):
        acc = acc + a_ref[s, 32:64, :].astype(F32)
    total_ref[...] = acc


def last_kernel(own_ref, one_ref, two_ref, rest_ref, c_ref, slots_s):
    group = lax.axis_index("rep") // (2 * NEAR)
    for k, ref in enumerate((own_ref, one_ref, two_ref)):
        slots_s[lax.rem(group + 3 - k, 3)] = ref[...]
    total = (slots_s[0] + slots_s[1] + slots_s[2]).astype(BF)
    for o in range(OWNERS):
        c_ref[o, 0:32, :] = rest_ref[o]
        c_ref[o, 32:64, :] = total


def collect_kernel(cuts, index_ref, *refs):
    *in_refs, out_ref, acc_s = refs
    acc_s[...] = jnp.zeros_like(acc_s)

    def body(s, carry):
        for ref, pieces in zip(in_refs, cuts):
            for slot, at, to, rows in pieces:
                i = index_ref[2 * s + slot]
                acc_s[i, to : to + rows, :] += ref[s, at : at + rows, :].astype(F32)
        return carry

    lax.fori_loop(0, OWNERS, body, 0, unroll=4)
    for i in range(TRASH):
        out_ref[RB * i : RB * i + RB, :HALF] = acc_s[i, 0:32, :].astype(BF)
        out_ref[RB * i : RB * i + RB, HALF:] = acc_s[i, 32:64, :].astype(BF)


def unpack_kernel(mine_ref, other_ref, self_ref, inter_ref):
    even = lax.rem(lax.axis_index("rep"), 2) == 0
    for o in range(OWNERS):
        mine = mine_ref[o, 32:64, :].astype(F32)
        other = other_ref[o].astype(F32)
        a = jnp.where(even, mine, other)
        b = jnp.where(even, other, mine)
        rows = slice(8 * o, 8 * o + 8)
        for ref, value in ((self_ref, a), (inter_ref, b)):
            ref[1, rows, :HALF] = value[0:8]
            ref[1, rows, HALF:] = value[8:16]
            ref[0, rows, :HALF] = value[16:24]
            ref[0, rows, HALF:] = value[24:32]


def call(kernel, outs, in_specs, scratch=(), params=PARAMS, **cost):
    return pl.pallas_call(
        kernel,
        out_shape=[jax.ShapeDtypeStruct(s, d) for s, d in outs],
        in_specs=in_specs,
        out_specs=[VMEM] * len(outs),
        scratch_shapes=list(scratch),
        compiler_params=params,
        cost_estimate=pl.CostEstimate(transcendentals=0, **cost),
    )


def local(cotangent, pre_two, pre_one, message_two, message_one, users_zero, w_self, w_inter, adjacency, tile_user,
          counts, dest, item_block):
    users = cotangent.shape[0]
    reps = lax.axis_size("rep")
    z_chips = reps // 2
    swap = [(i, i ^ 1) for i in range(reps)]
    dest = dest.reshape(dest.shape[0])

    def from_z(x, source):
        return lax.ppermute(x, "rep", [(2 * source(z) + c, 2 * z + c) for z in range(z_chips) for c in range(2)])

    def to_owners(x):
        return lax.all_to_all(x, "owner", split_axis=0, concat_axis=0, tiled=True)

    def rows(n):
        return ((OWNERS, n, HALF), BF)

    user = ((users, FEAT), BF)
    both = ((2, FEAT, FEAT), F32)
    chunk = ((32, HALF), F32)
    ranks = [pltpu.SMEM((OWNERS,), jnp.int32)] * 2
    small = dict(flops=1_000_000, bytes_accessed=2 << 20)
    tile = dict(flops=140_000_000, bytes_accessed=2 << 20)
    dmsg2, dmsg1, user_grad, keep, send = call(
        user_kernel,
        [user, user, user, both, (both[0], BF)],
        [HBM] * 8,
        [pltpu.VMEM((users, FEAT), BF)] * 6 + [pltpu.VMEM((2, FEAT, FEAT), BF)] * 2
        + [pltpu.VMEM((users, FEAT), BF)] * 6 + [pltpu.SemaphoreType.DMA((8 + 6 * (users // BLK),))],
        params=WIDE, flops=900_000_000, bytes_accessed=6 << 20,
    )(cotangent, pre_two, pre_one, message_two, message_one, users_zero, w_self, w_inter)
    got = lax.ppermute(send, "rep", swap)
    two, index_rows = call(
        two_kernel, [((2, OWNERS, 64, HALF), BF), rows(8)], [SMEM] * 4 + [VMEM] * 2,
        ranks + [pltpu.SMEM((2 * OWNERS,), jnp.int32)], **tile,
    )(tile_user, counts, dest, item_block, adjacency, dmsg2)
    (a,) = call(pack_kernel, [rows(64)], [VMEM] * 3, **small)(two, keep, got)
    got_a = to_owners(a)

    b, rest = call(
        one_kernel, [rows(200), rows(32)], [SMEM] * 3 + [VMEM] * 4,
        [pltpu.VMEM((2, OWNERS, 64, HALF), BF)] + ranks, **tile,
    )(tile_user, counts, dest, adjacency, dmsg1, two, index_rows)
    b, got_a = lax.optimization_barrier((b, got_a))
    got_b = to_owners(b)

    (total,) = call(chunk_kernel, [chunk], [VMEM], **small)(got_a)
    total = total + from_z(total, lambda z: z ^ 1)
    total = total + from_z(total, lambda z: z ^ 2)
    far = [from_z(total, lambda z, k=k: (z + z_chips - NEAR * k) % z_chips) for k in (1, 2)]
    (c,) = call(last_kernel, [rows(64)], [VMEM] * 4, [pltpu.VMEM((3, 32, HALF), F32)], **small)(total, *far, rest)
    c, got_b = lax.optimization_barrier((c, got_b))
    got_c = to_owners(c)

    index = got_b[:, 192:200:4, 0].astype(jnp.int32).reshape(2 * OWNERS)

    def collect(cuts, *arrays):
        return call(
            functools.partial(collect_kernel, cuts), [((OWNERS * RB, FEAT), BF)], [SMEM] + [VMEM] * len(arrays),
            [pltpu.VMEM((TRASH + 1, 64, HALF), F32)], **small,
        )(index, *arrays)[0]

    item_one = collect((((0, 0, 0, 32),), ((0, 0, 32, 32), (1, 32, 0, 64))), got_a, got_b)
    got_c, item_one = lax.optimization_barrier((got_c, item_one))
    other = lax.ppermute(got_c[:, 32:64], "rep", swap)
    item_zero = collect((((0, 96, 0, 64), (1, 160, 0, 32)), ((1, 0, 32, 32),)), got_b, got_c)
    self_grad, inter_grad = call(unpack_kernel, [both] * 2, [VMEM] * 2, **small)(got_c, other)
    return user_grad, item_one, item_zero, self_grad, inter_grad


def solution(mesh):
    both = ("owner", "rep")
    rows = P(both, None)
    return jax.shard_map(
        local,
        mesh=mesh,
        in_specs=(rows,) * 6 + (P(), P(), P(both, None, None), P(both), P(both), rows, P(both)),
        out_specs=(rows, rows, rows, P(), P()),
        check_vma=False,
    )
```

```python
import functools

import functools

import jax
import jax.numpy as jnp
from jax import lax
from jax.experimental import pallas as pl
from jax.experimental.pallas import tpu as pltpu
from jax.sharding import PartitionSpec as P

BF = jnp.bfloat16
F32 = jnp.float32
SLOPE = 0.2
RB = 32
FEAT = 256
HALF = 128
BLK = 256
OWNERS = 32
XS = 4
YS = 8
INDEX = 256
TRASH = 32
NEAR = 4
VMEM = pl.BlockSpec(memory_space=pltpu.VMEM)
SMEM = pl.BlockSpec(memory_space=pltpu.SMEM)
HBM = pl.BlockSpec(memory_space=pltpu.HBM)
PARAMS = pltpu.CompilerParams(vmem_limit_bytes=12 * 1024 * 1024)
WIDE = pltpu.CompilerParams(vmem_limit_bytes=60 * 1024 * 1024)


def tdot(a, b):
    return lax.dot_general(a, b, (((0,), (0,)), ((), ())), preferred_element_type=F32)


def dot_t(a, b):
    return lax.dot_general(a, b, (((1,), (1,)), ((), ())), preferred_element_type=F32)


def user_kernel(*refs):
    ins, rest = refs[:8], refs[8:]
    dmsg2_ref, dmsg1_ref, user_grad_ref, keep_ref, send_ref = rest[:5]
    bufs, sum2_s, prod2_s, delta2_s, sum1_s, prod1_s, delta1_s, sems = rest[5:13], *rest[13:]
    blocks = ins[0].shape[0] // BLK
    weights = [pltpu.make_async_copy(ins[i], bufs[i], sems.at[i]) for i in (6, 7)]
    for copy in weights:
        copy.start()
    loads = []
    for b in range(blocks):
        rows = pl.ds(b * BLK, BLK)
        loads.append(
            [pltpu.make_async_copy(ins[i].at[rows], bufs[i].at[rows], sems.at[8 + 6 * b + i]) for i in range(6)]
        )
        for copy in loads[-1]:
            copy.start()
    cot, pre2, pre1, msg2, msg1, zero, ws, wi = bufs
    for copy in weights:
        copy.wait()
    for b in range(blocks):
        rows = pl.ds(b * BLK, BLK)
        for copy in loads[b]:
            copy.wait()
        one = pre1[rows, :].astype(F32)
        prev = jnp.where(one > 0, one, SLOPE * one).astype(BF).astype(F32)
        deltas = (cot[rows, :].astype(F32) * jnp.where(pre2[rows, :].astype(F32) > 0, 1.0, SLOPE)).astype(BF)
        msg = msg2[rows, :].astype(F32)
        delta2_s[rows, :] = deltas
        sum2_s[rows, :] = (msg + prev).astype(BF)
        prod2_s[rows, :] = (msg * prev).astype(BF)
        back_self = dot_t(deltas, ws[1])
        back_inter = dot_t(deltas, wi[1])
        dmsg2_ref[rows, :] = (back_self + back_inter * prev).astype(BF)
        dprev = back_self + back_inter * msg
        deltas = (dprev * jnp.where(one > 0, 1.0, SLOPE)).astype(BF)
        msg = msg1[rows, :].astype(F32)
        prev = zero[rows, :].astype(F32)
        delta1_s[rows, :] = deltas
        sum1_s[rows, :] = (msg + prev).astype(BF)
        prod1_s[rows, :] = (msg * prev).astype(BF)
        back_self = dot_t(deltas, ws[0])
        back_inter = dot_t(deltas, wi[0])
        dmsg1_ref[rows, :] = (back_self + back_inter * prev).astype(BF)
        user_grad_ref[rows, :] = (back_self + back_inter * msg).astype(BF)
    even = lax.rem(lax.axis_index("rep"), 2) == 0
    for at, (sum_s, prod_s, delta_s) in enumerate(((sum2_s, prod2_s, delta2_s), (sum1_s, prod1_s, delta1_s))):
        grad_self = tdot(sum_s[...], delta_s[...])
        grad_inter = tdot(prod_s[...], delta_s[...])
        keep_ref[at] = jnp.where(even, grad_self, grad_inter)
        send_ref[at] = jnp.where(even, grad_inter, grad_self).astype(BF)


def rank_blocks(dest_ref, rank_s, seen_s):
    for o in range(OWNERS):
        seen_s[o] = 0
    for j in range(dest_ref.shape[0]):
        o = dest_ref[j]
        rank_s[j] = seen_s[o]
        seen_s[o] = seen_s[o] + 1


def tile_terms(user_ref, count_ref, dest_ref, adj_ref, dmsg_ref, rank_s, out_ref):
    for t in range(adj_ref.shape[0]):
        start = pl.multiple_of(user_ref[t] * BLK, BLK)
        part = tdot(adj_ref[t], dmsg_ref[pl.ds(start, BLK), :])
        live = lax.broadcasted_iota(jnp.int32, part.shape, 0) < count_ref[t]
        part = jnp.where(live, part, 0.0).astype(BF)
        for b in range(part.shape[0] // RB):
            j = t * (part.shape[0] // RB) + b
            block = part[b * RB : (b + 1) * RB, :]
            out_ref[rank_s[j], dest_ref[j], 0:32, :] = block[:, :HALF]
            out_ref[rank_s[j], dest_ref[j], 32:64, :] = block[:, HALF:]


def two_kernel(user_ref, count_ref, dest_ref, item_ref, adj_ref, dmsg_ref, slots_ref, index_ref, rank_s, seen_s, tab_s):
    rank_blocks(dest_ref, rank_s, seen_s)
    for i in range(2 * OWNERS):
        tab_s[i] = TRASH
    for j in range(dest_ref.shape[0]):
        tab_s[2 * dest_ref[j] + rank_s[j]] = item_ref[j]
    slots_ref[...] = jnp.zeros_like(slots_ref)
    top = lax.broadcasted_iota(jnp.int32, (8, HALF), 0) < 4
    for o in range(OWNERS):
        index_ref[o] = jnp.where(top, tab_s[2 * o], tab_s[2 * o + 1]).astype(F32).astype(BF)
    tile_terms(user_ref, count_ref, dest_ref, adj_ref, dmsg_ref, rank_s, slots_ref)


def one_kernel(user_ref, count_ref, dest_ref, adj_ref, dmsg_ref, two_ref, index_ref, b_ref, slots_s, rank_s, seen_s):
    rank_blocks(dest_ref, rank_s, seen_s)
    slots_s[...] = jnp.zeros_like(slots_s)
    tile_terms(user_ref, count_ref, dest_ref, adj_ref, dmsg_ref, rank_s, slots_s)
    for o in range(OWNERS):
        for slot in range(2):
            b_ref[o, 64 * slot : 64 * slot + 64, :] = two_ref[slot, o]
            b_ref[o, 128 + 64 * slot : 192 + 64 * slot, :] = slots_s[slot, o]
        b_ref[o, INDEX : INDEX + 8, :] = index_ref[o]


def pack_kernel(keep_ref, got_ref, a_ref):
    for y in range(YS):
        for at in range(2):
            rows = slice(32 * y, 32 * y + 32)
            total = keep_ref[at, rows, :] + got_ref[at, rows, :].astype(F32)
            a_ref[y, 64 * at : 64 * at + 32, :] = total[:, :HALF].astype(BF)
            a_ref[y, 64 * at + 32 : 64 * at + 64, :] = total[:, HALF:].astype(BF)


def chunk_kernel(a_ref, total_ref):
    acc = a_ref[0].astype(F32)
    for y in range(1, YS):
        acc = acc + a_ref[y].astype(F32)
    total_ref[...] = acc


def last_kernel(own_ref, one_ref, two_ref, c_ref, slots_s):
    group = lax.axis_index("rep") // (2 * NEAR)
    for k, ref in enumerate((own_ref, one_ref, two_ref)):
        slots_s[lax.rem(group + 3 - k, 3)] = ref[...]
    total = (slots_s[0] + slots_s[1] + slots_s[2]).astype(BF)
    for y in range(YS):
        c_ref[y] = total


def collect_kernel(cuts, index_ref, *refs):
    *in_refs, out_ref, acc_s = refs
    acc_s[...] = jnp.zeros_like(acc_s)

    def body(s, carry):
        for ref, pieces in zip(in_refs, cuts):
            for slot, at, to, rows in pieces:
                i = index_ref[2 * s + slot]
                acc_s[i, to : to + rows, :] += ref[s, at : at + rows, :].astype(F32)
        return carry

    lax.fori_loop(0, OWNERS, body, 0, unroll=4)
    for i in range(TRASH):
        out_ref[RB * i : RB * i + RB, :HALF] = acc_s[i, 0:32, :].astype(BF)
        out_ref[RB * i : RB * i + RB, HALF:] = acc_s[i, 32:64, :].astype(BF)


def unpack_kernel(mine_ref, other_ref, self_ref, inter_ref):
    even = lax.rem(lax.axis_index("rep"), 2) == 0
    for y in range(YS):
        mine = mine_ref[y].astype(F32)
        other = other_ref[y].astype(F32)
        rows = slice(32 * y, 32 * y + 32)
        for ref, value in ((self_ref, jnp.where(even, mine, other)), (inter_ref, jnp.where(even, other, mine))):
            for at, layer in ((0, 1), (64, 0)):
                ref[layer, rows, :HALF] = value[at : at + 32]
                ref[layer, rows, HALF:] = value[at + 32 : at + 64]


def call(kernel, outs, in_specs, scratch=(), params=PARAMS, **cost):
    return pl.pallas_call(
        kernel,
        out_shape=[jax.ShapeDtypeStruct(s, d) for s, d in outs],
        in_specs=in_specs,
        out_specs=[VMEM] * len(outs),
        scratch_shapes=list(scratch),
        compiler_params=params,
        cost_estimate=pl.CostEstimate(transcendentals=0, **cost),
    )


def local(cotangent, pre_two, pre_one, message_two, message_one, users_zero, w_self, w_inter, adjacency, tile_user,
          counts, dest, item_block):
    users = cotangent.shape[0]
    reps = lax.axis_size("rep")
    z_chips = reps // 2
    swap = [(i, i ^ 1) for i in range(reps)]
    dest = dest.reshape(dest.shape[0])

    def from_z(x, source):
        return lax.ppermute(x, "rep", [(2 * source(z) + c, 2 * z + c) for z in range(z_chips) for c in range(2)])

    def to_owners(x):
        return lax.all_to_all(x, "owner", split_axis=0, concat_axis=0, tiled=True)

    def to_column(x):
        columns = [[XS * y + x for y in range(YS)] for x in range(XS)]
        return lax.all_to_all(x, "owner", split_axis=0, concat_axis=0, tiled=True, axis_index_groups=columns)

    def add_x(x, bit):
        return x + lax.ppermute(x, "owner", [(o, o ^ bit) for o in range(OWNERS)])

    def rows(n, lead=OWNERS):
        return ((lead, n, HALF), BF)

    user = ((users, FEAT), BF)
    both = ((2, FEAT, FEAT), F32)
    chunk = ((128, HALF), F32)
    ranks = [pltpu.SMEM((OWNERS,), jnp.int32)] * 2
    small = dict(flops=1_000_000, bytes_accessed=2 << 20)
    tile = dict(flops=140_000_000, bytes_accessed=2 << 20)
    dmsg2, dmsg1, user_grad, keep, send = call(
        user_kernel,
        [user, user, user, both, (both[0], BF)],
        [HBM] * 8,
        [pltpu.VMEM((users, FEAT), BF)] * 6 + [pltpu.VMEM((2, FEAT, FEAT), BF)] * 2
        + [pltpu.VMEM((users, FEAT), BF)] * 6 + [pltpu.SemaphoreType.DMA((8 + 6 * (users // BLK),))],
        params=WIDE, flops=900_000_000, bytes_accessed=6 << 20,
    )(cotangent, pre_two, pre_one, message_two, message_one, users_zero, w_self, w_inter)
    got = lax.ppermute(send, "rep", swap)
    two, index_rows = call(
        two_kernel, [((2, OWNERS, 64, HALF), BF), rows(8)], [SMEM] * 4 + [VMEM] * 2,
        ranks + [pltpu.SMEM((2 * OWNERS,), jnp.int32)], **tile,
    )(tile_user, counts, dest, item_block, adjacency, dmsg2)
    (a,) = call(pack_kernel, [rows(128, YS)], [VMEM] * 2, **small)(keep, got)
    got_a = to_column(a)

    (b,) = call(
        one_kernel, [rows(INDEX + 8)], [SMEM] * 3 + [VMEM] * 4,
        [pltpu.VMEM((2, OWNERS, 64, HALF), BF)] + ranks, **tile,
    )(tile_user, counts, dest, adjacency, dmsg1, two, index_rows)
    b, got_a = lax.optimization_barrier((b, got_a))
    got_b = to_owners(b)

    (total,) = call(chunk_kernel, [chunk], [VMEM], **small)(got_a)
    total = add_x(add_x(total, 1), 2)
    total = total + from_z(total, lambda z: z ^ 1)
    total = total + from_z(total, lambda z: z ^ 2)
    far = [from_z(total, lambda z, k=k: (z + z_chips - NEAR * k) % z_chips) for k in (1, 2)]
    (c,) = call(last_kernel, [rows(128, YS)], [VMEM] * 3, [pltpu.VMEM((3, 128, HALF), F32)], **small)(total, *far)
    c, got_b = lax.optimization_barrier((c, got_b))
    got_c = to_column(c)

    index = got_b[:, INDEX : INDEX + 8 : 4, 0].astype(jnp.int32).reshape(2 * OWNERS)

    def collect(cuts, *arrays):
        return call(
            functools.partial(collect_kernel, cuts), [((OWNERS * RB, FEAT), BF)], [SMEM] + [VMEM] * len(arrays),
            [pltpu.VMEM((TRASH + 1, 64, HALF), F32)], **small,
        )(index, *arrays)[0]

    item_one = collect((((0, 0, 0, 64), (1, 64, 0, 64)),), got_b)
    item_zero = collect((((0, 128, 0, 64), (1, 192, 0, 64)),), got_b)
    got_c, item_one, item_zero = lax.optimization_barrier((got_c, item_one, item_zero))
    other = lax.ppermute(got_c, "rep", swap)
    self_grad, inter_grad = call(unpack_kernel, [both] * 2, [VMEM] * 2, **small)(got_c, other)
    return user_grad, item_one, item_zero, self_grad, inter_grad


def solution(mesh):
    both = ("owner", "rep")
    rows = P(both, None)
    return jax.shard_map(
        local,
        mesh=mesh,
        in_specs=(rows,) * 6 + (P(), P(), P(both, None, None), P(both), P(both), rows, P(both)),
        out_specs=(rows, rows, rows, P(), P()),
        check_vma=False,
    )
```

```python
import functools

import functools

import jax
import jax.numpy as jnp
from jax import lax
from jax.experimental import pallas as pl
from jax.experimental.pallas import tpu as pltpu
from jax.sharding import PartitionSpec as P

BF = jnp.bfloat16
F32 = jnp.float32
SLOPE = 0.2
RB = 32
FEAT = 256
HALF = 128
BLK = 256
OWNERS = 32
TRASH = 32
NEAR = 4
VMEM = pl.BlockSpec(memory_space=pltpu.VMEM)
SMEM = pl.BlockSpec(memory_space=pltpu.SMEM)
HBM = pl.BlockSpec(memory_space=pltpu.HBM)
PARAMS = pltpu.CompilerParams(vmem_limit_bytes=12 * 1024 * 1024)
WIDE = pltpu.CompilerParams(vmem_limit_bytes=60 * 1024 * 1024)


def tdot(a, b):
    return lax.dot_general(a, b, (((0,), (0,)), ((), ())), preferred_element_type=F32)


def dot_t(a, b):
    return lax.dot_general(a, b, (((1,), (1,)), ((), ())), preferred_element_type=F32)


def user_kernel(*refs):
    ins, rest = refs[:8], refs[8:]
    near_ref, dmsg1_ref, user_grad_ref, send_ref = rest[:4]
    bufs, sum2_s, prod2_s, delta2_s, sum1_s, prod1_s, delta1_s, sems = rest[4:12], *rest[12:]
    users = ins[0].shape[0]
    blocks = users // BLK
    weights = [pltpu.make_async_copy(ins[i], bufs[i], sems.at[i]) for i in (6, 7)]
    for copy in weights:
        copy.start()
    loads = []
    for b in range(blocks):
        rows = pl.ds(b * BLK, BLK)
        loads.append(
            [pltpu.make_async_copy(ins[i].at[rows], bufs[i].at[rows], sems.at[8 + 6 * b + i]) for i in range(6)]
        )
        for copy in loads[-1]:
            copy.start()
    cot, pre2, pre1, msg2, msg1, zero, ws, wi = bufs
    for copy in weights:
        copy.wait()
    for b in range(blocks):
        rows = pl.ds(b * BLK, BLK)
        for copy in loads[b]:
            copy.wait()
        one = pre1[rows, :].astype(F32)
        prev = jnp.where(one > 0, one, SLOPE * one).astype(BF).astype(F32)
        deltas = (cot[rows, :].astype(F32) * jnp.where(pre2[rows, :].astype(F32) > 0, 1.0, SLOPE)).astype(BF)
        msg = msg2[rows, :].astype(F32)
        delta2_s[rows, :] = deltas
        sum2_s[rows, :] = (msg + prev).astype(BF)
        prod2_s[rows, :] = (msg * prev).astype(BF)
        back_self = dot_t(deltas, ws[1])
        back_inter = dot_t(deltas, wi[1])
        near_ref[rows, :] = (back_self + back_inter * prev).astype(BF)
        dprev = back_self + back_inter * msg
        deltas = (dprev * jnp.where(one > 0, 1.0, SLOPE)).astype(BF)
        msg = msg1[rows, :].astype(F32)
        prev = zero[rows, :].astype(F32)
        delta1_s[rows, :] = deltas
        sum1_s[rows, :] = (msg + prev).astype(BF)
        prod1_s[rows, :] = (msg * prev).astype(BF)
        back_self = dot_t(deltas, ws[0])
        back_inter = dot_t(deltas, wi[0])
        dmsg1_ref[rows, :] = (back_self + back_inter * prev).astype(BF)
        user_grad_ref[rows, :] = (back_self + back_inter * msg).astype(BF)
    even = lax.rem(lax.axis_index("rep"), 2) == 0
    for at, (sum_s, prod_s, delta_s) in enumerate(((sum2_s, prod2_s, delta2_s), (sum1_s, prod1_s, delta1_s))):
        grad_self = tdot(sum_s[...], delta_s[...])
        grad_inter = tdot(prod_s[...], delta_s[...])
        near_ref[users + at * FEAT : users + (at + 1) * FEAT, :] = jnp.where(even, grad_self, grad_inter).astype(BF)
        send_ref[at] = jnp.where(even, grad_inter, grad_self).astype(BF)


def rank_blocks(dest_ref, rank_s, seen_s):
    for o in range(OWNERS):
        seen_s[o] = 0
    for j in range(dest_ref.shape[0]):
        o = dest_ref[j]
        rank_s[j] = seen_s[o]
        seen_s[o] = seen_s[o] + 1


def tile_terms(user_ref, count_ref, dest_ref, adj_ref, dmsg_ref, rank_s, out_ref):
    for t in range(adj_ref.shape[0]):
        start = pl.multiple_of(user_ref[t] * BLK, BLK)
        part = tdot(adj_ref[t], dmsg_ref[pl.ds(start, BLK), :])
        live = lax.broadcasted_iota(jnp.int32, part.shape, 0) < count_ref[t]
        part = jnp.where(live, part, 0.0).astype(BF)
        for b in range(part.shape[0] // RB):
            j = t * (part.shape[0] // RB) + b
            block = part[b * RB : (b + 1) * RB, :]
            out_ref[rank_s[j], dest_ref[j], 0:32, :] = block[:, :HALF]
            out_ref[rank_s[j], dest_ref[j], 32:64, :] = block[:, HALF:]


def two_kernel(user_ref, count_ref, dest_ref, item_ref, adj_ref, dmsg_ref, slots_ref, index_ref, rank_s, seen_s, tab_s):
    rank_blocks(dest_ref, rank_s, seen_s)
    for i in range(2 * OWNERS):
        tab_s[i] = TRASH
    for j in range(dest_ref.shape[0]):
        tab_s[2 * dest_ref[j] + rank_s[j]] = item_ref[j]
    slots_ref[...] = jnp.zeros_like(slots_ref)
    top = lax.broadcasted_iota(jnp.int32, (8, HALF), 0) < 4
    for o in range(OWNERS):
        index_ref[o] = jnp.where(top, tab_s[2 * o], tab_s[2 * o + 1]).astype(F32).astype(BF)
    tile_terms(user_ref, count_ref, dest_ref, adj_ref, dmsg_ref, rank_s, slots_ref)


def one_kernel(user_ref, count_ref, dest_ref, adj_ref, dmsg_ref, two_ref, index_ref, b_ref, rest_ref, slots_s, rank_s,
               seen_s):
    rank_blocks(dest_ref, rank_s, seen_s)
    slots_s[...] = jnp.zeros_like(slots_s)
    tile_terms(user_ref, count_ref, dest_ref, adj_ref, dmsg_ref, rank_s, slots_s)
    for o in range(OWNERS):
        b_ref[o, 0:32, :] = two_ref[0, o, 32:64, :]
        b_ref[o, 32:96, :] = two_ref[1, o]
        b_ref[o, 96:160, :] = slots_s[0, o]
        b_ref[o, 160:192, :] = slots_s[1, o, 0:32, :]
        b_ref[o, 192:200, :] = index_ref[o]
        rest_ref[o] = slots_s[1, o, 32:64, :]


def pack_kernel(two_ref, near_ref, got_ref, a_ref):
    kept = near_ref.shape[0] - got_ref.shape[0] * FEAT
    for o in range(0, OWNERS, 2):
        for p in range(2):
            a_ref[o + p, 0:32, :] = two_ref[0, o + p, 0:32, :]
        for at in range(2):
            first = kept + at * FEAT + 8 * o
            total = near_ref[first : first + 16, :].astype(F32) + got_ref[at, 8 * o : 8 * o + 16, :].astype(F32)
            for p in range(2):
                part = total[8 * p : 8 * p + 8, :]
                part = jnp.concatenate([part[:, :HALF], part[:, HALF:]], axis=0)
                a_ref[o + p, 32 + 16 * at : 48 + 16 * at, :] = part.astype(BF)


def chunk_kernel(a_ref, total_ref):
    acc = a_ref[0, 32:64, :].astype(F32)
    for s in range(1, OWNERS):
        acc = acc + a_ref[s, 32:64, :].astype(F32)
    total_ref[...] = acc


def last_kernel(own_ref, one_ref, two_ref, rest_ref, c_ref, slots_s):
    group = lax.axis_index("rep") // (2 * NEAR)
    for k, ref in enumerate((own_ref, one_ref, two_ref)):
        slots_s[lax.rem(group + 3 - k, 3)] = ref[...]
    total = (slots_s[0] + slots_s[1] + slots_s[2]).astype(BF)
    for o in range(OWNERS):
        c_ref[o, 0:32, :] = rest_ref[o]
        c_ref[o, 32:64, :] = total


def collect_kernel(cuts, index_ref, *refs):
    *in_refs, out_ref, acc_s = refs
    acc_s[...] = jnp.zeros_like(acc_s)

    def body(s, carry):
        for ref, pieces in zip(in_refs, cuts):
            for slot, at, to, rows in pieces:
                i = index_ref[2 * s + slot]
                acc_s[i, to : to + rows, :] += ref[s, at : at + rows, :].astype(F32)
        return carry

    lax.fori_loop(0, OWNERS, body, 0, unroll=4)
    for i in range(TRASH):
        out_ref[RB * i : RB * i + RB, :HALF] = acc_s[i, 0:32, :].astype(BF)
        out_ref[RB * i : RB * i + RB, HALF:] = acc_s[i, 32:64, :].astype(BF)


def unpack_kernel(mine_ref, other_ref, self_ref, inter_ref):
    even = lax.rem(lax.axis_index("rep"), 2) == 0
    for o in range(OWNERS):
        mine = mine_ref[o, 32:64, :].astype(F32)
        other = other_ref[o].astype(F32)
        a = jnp.where(even, mine, other)
        b = jnp.where(even, other, mine)
        rows = slice(8 * o, 8 * o + 8)
        for ref, value in ((self_ref, a), (inter_ref, b)):
            ref[1, rows, :HALF] = value[0:8]
            ref[1, rows, HALF:] = value[8:16]
            ref[0, rows, :HALF] = value[16:24]
            ref[0, rows, HALF:] = value[24:32]


def call(kernel, outs, in_specs, scratch=(), params=PARAMS, **cost):
    return pl.pallas_call(
        kernel,
        out_shape=[jax.ShapeDtypeStruct(s, d) for s, d in outs],
        in_specs=in_specs,
        out_specs=[VMEM] * len(outs),
        scratch_shapes=list(scratch),
        compiler_params=params,
        cost_estimate=pl.CostEstimate(transcendentals=0, **cost),
    )


def local(cotangent, pre_two, pre_one, message_two, message_one, users_zero, w_self, w_inter, adjacency, tile_user,
          counts, dest, item_block):
    users = cotangent.shape[0]
    reps = lax.axis_size("rep")
    z_chips = reps // 2
    swap = [(i, i ^ 1) for i in range(reps)]
    dest = dest.reshape(dest.shape[0])

    def from_z(x, source):
        return lax.ppermute(x, "rep", [(2 * source(z) + c, 2 * z + c) for z in range(z_chips) for c in range(2)])

    def to_owners(x):
        return lax.all_to_all(x, "owner", split_axis=0, concat_axis=0, tiled=True)

    def rows(n):
        return ((OWNERS, n, HALF), BF)

    user = ((users, FEAT), BF)
    both = ((2, FEAT, FEAT), F32)
    chunk = ((32, HALF), F32)
    ranks = [pltpu.SMEM((OWNERS,), jnp.int32)] * 2
    small = dict(flops=1_000_000, bytes_accessed=2 << 20)
    tile = dict(flops=140_000_000, bytes_accessed=2 << 20)
    near, dmsg1, user_grad, send = call(
        user_kernel,
        [((users + 2 * FEAT, FEAT), BF), user, user, (both[0], BF)],
        [HBM] * 8,
        [pltpu.VMEM((users, FEAT), BF)] * 6 + [pltpu.VMEM((2, FEAT, FEAT), BF)] * 2
        + [pltpu.VMEM((users, FEAT), BF)] * 6 + [pltpu.SemaphoreType.DMA((8 + 6 * (users // BLK),))],
        params=WIDE, flops=900_000_000, bytes_accessed=6 << 20,
    )(cotangent, pre_two, pre_one, message_two, message_one, users_zero, w_self, w_inter)
    got = lax.ppermute(send, "rep", swap)
    two, index_rows = call(
        two_kernel, [((2, OWNERS, 64, HALF), BF), rows(8)], [SMEM] * 4 + [VMEM] * 2,
        ranks + [pltpu.SMEM((2 * OWNERS,), jnp.int32)], **tile,
    )(tile_user, counts, dest, item_block, adjacency, near)
    (a,) = call(pack_kernel, [rows(64)], [VMEM] * 3, **small)(two, near, got)
    got_a = to_owners(a)

    b, rest = call(
        one_kernel, [rows(200), rows(32)], [SMEM] * 3 + [VMEM] * 4,
        [pltpu.VMEM((2, OWNERS, 64, HALF), BF)] + ranks, **tile,
    )(tile_user, counts, dest, adjacency, dmsg1, two, index_rows)
    b, got_a = lax.optimization_barrier((b, got_a))
    got_b = to_owners(b)

    (total,) = call(chunk_kernel, [chunk], [VMEM], **small)(got_a)
    total = total + from_z(total, lambda z: z ^ 1)
    total = total + from_z(total, lambda z: z ^ 2)
    far = [from_z(total, lambda z, k=k: (z + z_chips - NEAR * k) % z_chips) for k in (1, 2)]
    (c,) = call(last_kernel, [rows(64)], [VMEM] * 4, [pltpu.VMEM((3, 32, HALF), F32)], **small)(total, *far, rest)
    c, got_b = lax.optimization_barrier((c, got_b))
    got_c = to_owners(c)

    index = got_b[:, 192:200:4, 0].astype(jnp.int32).reshape(2 * OWNERS)

    def collect(cuts, *arrays):
        return call(
            functools.partial(collect_kernel, cuts), [((OWNERS * RB, FEAT), BF)], [SMEM] + [VMEM] * len(arrays),
            [pltpu.VMEM((TRASH + 1, 64, HALF), F32)], **small,
        )(index, *arrays)[0]

    item_one = collect((((0, 0, 0, 32),), ((0, 0, 32, 32), (1, 32, 0, 64))), got_a, got_b)
    got_c, item_one = lax.optimization_barrier((got_c, item_one))
    other = lax.ppermute(got_c[:, 32:64], "rep", swap)
    item_zero = collect((((0, 96, 0, 64), (1, 160, 0, 32)), ((1, 0, 32, 32),)), got_b, got_c)
    self_grad, inter_grad = call(unpack_kernel, [both] * 2, [VMEM] * 2, **small)(got_c, other)
    return user_grad, item_one, item_zero, self_grad, inter_grad


def solution(mesh):
    both = ("owner", "rep")
    rows = P(both, None)
    return jax.shard_map(
        local,
        mesh=mesh,
        in_specs=(rows,) * 6 + (P(), P(), P(both, None, None), P(both), P(both), rows, P(both)),
        out_specs=(rows, rows, rows, P(), P()),
        check_vma=False,
    )
```

```python
import functools

import functools

import jax
import jax.numpy as jnp
from jax import lax
from jax.experimental import pallas as pl
from jax.experimental.pallas import tpu as pltpu
from jax.sharding import PartitionSpec as P

BF = jnp.bfloat16
F32 = jnp.float32
SLOPE = 0.2
RB = 32
FEAT = 256
HALF = 128
BLK = 256
OWNERS = 32
TRASH = 32
NEAR = 4
VMEM = pl.BlockSpec(memory_space=pltpu.VMEM)
SMEM = pl.BlockSpec(memory_space=pltpu.SMEM)
HBM = pl.BlockSpec(memory_space=pltpu.HBM)
PARAMS = pltpu.CompilerParams(vmem_limit_bytes=12 * 1024 * 1024)
WIDE = pltpu.CompilerParams(vmem_limit_bytes=60 * 1024 * 1024)


def tdot(a, b):
    return lax.dot_general(a, b, (((0,), (0,)), ((), ())), preferred_element_type=F32)


def dot_t(a, b):
    return lax.dot_general(a, b, (((1,), (1,)), ((), ())), preferred_element_type=F32)


def user_kernel(*refs):
    ins, rest = refs[:8], refs[8:]
    dmsg2_ref, dmsg1_ref, user_grad_ref, a_ref = rest[:4]
    bufs, sum2_s, prod2_s, delta2_s, sum1_s, prod1_s, delta1_s, sems = rest[4:12], *rest[12:]
    users = ins[0].shape[0]
    blocks = users // BLK
    weights = [pltpu.make_async_copy(ins[i], bufs[i], sems.at[i]) for i in (6, 7)]
    for copy in weights:
        copy.start()
    loads = []
    for b in range(blocks):
        rows = pl.ds(b * BLK, BLK)
        loads.append(
            [pltpu.make_async_copy(ins[i].at[rows], bufs[i].at[rows], sems.at[8 + 6 * b + i]) for i in range(6)]
        )
        for copy in loads[-1]:
            copy.start()
    cot, pre2, pre1, msg2, msg1, zero, ws, wi = bufs
    for copy in weights:
        copy.wait()
    for b in range(blocks):
        rows = pl.ds(b * BLK, BLK)
        for copy in loads[b]:
            copy.wait()
        one = pre1[rows, :].astype(F32)
        prev = jnp.where(one > 0, one, SLOPE * one).astype(BF).astype(F32)
        deltas = (cot[rows, :].astype(F32) * jnp.where(pre2[rows, :].astype(F32) > 0, 1.0, SLOPE)).astype(BF)
        msg = msg2[rows, :].astype(F32)
        delta2_s[rows, :] = deltas
        sum2_s[rows, :] = (msg + prev).astype(BF)
        prod2_s[rows, :] = (msg * prev).astype(BF)
        back_self = dot_t(deltas, ws[1])
        back_inter = dot_t(deltas, wi[1])
        dmsg2_ref[rows, :] = (back_self + back_inter * prev).astype(BF)
        dprev = back_self + back_inter * msg
        deltas = (dprev * jnp.where(one > 0, 1.0, SLOPE)).astype(BF)
        msg = msg1[rows, :].astype(F32)
        prev = zero[rows, :].astype(F32)
        delta1_s[rows, :] = deltas
        sum1_s[rows, :] = (msg + prev).astype(BF)
        prod1_s[rows, :] = (msg * prev).astype(BF)
        back_self = dot_t(deltas, ws[0])
        back_inter = dot_t(deltas, wi[0])
        dmsg1_ref[rows, :] = (back_self + back_inter * prev).astype(BF)
        user_grad_ref[rows, :] = (back_self + back_inter * msg).astype(BF)
    for at, (sum_s, prod_s, delta_s) in enumerate(((sum2_s, prod2_s, delta2_s), (sum1_s, prod1_s, delta1_s))):
        for half, left_s in enumerate((sum_s, prod_s)):
            grad = tdot(left_s[...], delta_s[...])
            first = 32 * half + 16 * at
            for o in range(OWNERS):
                part = grad[8 * o : 8 * o + 8, :]
                part = jnp.concatenate([part[:, :HALF], part[:, HALF:]], axis=0)
                a_ref[o, first : first + 16, :] = part.astype(BF)


def rank_blocks(dest_ref, rank_s, seen_s):
    for o in range(OWNERS):
        seen_s[o] = 0
    for j in range(dest_ref.shape[0]):
        o = dest_ref[j]
        rank_s[j] = seen_s[o]
        seen_s[o] = seen_s[o] + 1


def tile_terms(user_ref, count_ref, dest_ref, adj_ref, dmsg_ref, rank_s, out_ref):
    for t in range(adj_ref.shape[0]):
        start = pl.multiple_of(user_ref[t] * BLK, BLK)
        part = tdot(adj_ref[t], dmsg_ref[pl.ds(start, BLK), :])
        live = lax.broadcasted_iota(jnp.int32, part.shape, 0) < count_ref[t]
        part = jnp.where(live, part, 0.0).astype(BF)
        for b in range(part.shape[0] // RB):
            j = t * (part.shape[0] // RB) + b
            block = part[b * RB : (b + 1) * RB, :]
            out_ref[rank_s[j], dest_ref[j], 0:32, :] = block[:, :HALF]
            out_ref[rank_s[j], dest_ref[j], 32:64, :] = block[:, HALF:]


def two_kernel(user_ref, count_ref, dest_ref, item_ref, adj_ref, dmsg_ref, slots_ref, index_ref, rank_s, seen_s, tab_s):
    rank_blocks(dest_ref, rank_s, seen_s)
    for i in range(2 * OWNERS):
        tab_s[i] = TRASH
    for j in range(dest_ref.shape[0]):
        tab_s[2 * dest_ref[j] + rank_s[j]] = item_ref[j]
    slots_ref[...] = jnp.zeros_like(slots_ref)
    top = lax.broadcasted_iota(jnp.int32, (8, HALF), 0) < 4
    for o in range(OWNERS):
        index_ref[o] = jnp.where(top, tab_s[2 * o], tab_s[2 * o + 1]).astype(F32).astype(BF)
    tile_terms(user_ref, count_ref, dest_ref, adj_ref, dmsg_ref, rank_s, slots_ref)


def one_kernel(user_ref, count_ref, dest_ref, adj_ref, dmsg_ref, two_ref, index_ref, b_ref, rest_ref, slots_s, rank_s,
               seen_s):
    rank_blocks(dest_ref, rank_s, seen_s)
    slots_s[...] = jnp.zeros_like(slots_s)
    tile_terms(user_ref, count_ref, dest_ref, adj_ref, dmsg_ref, rank_s, slots_s)
    for o in range(OWNERS):
        b_ref[o, 0:64, :] = two_ref[0, o]
        b_ref[o, 64:128, :] = two_ref[1, o]
        b_ref[o, 128:192, :] = slots_s[0, o]
        b_ref[o, 192:224, :] = slots_s[1, o, 0:32, :]
        b_ref[o, 224:232, :] = index_ref[o]
        rest_ref[o] = slots_s[1, o, 32:64, :]


def chunk_kernel(a_ref, keep_ref, send_ref):
    acc = a_ref[0].astype(F32)
    for s in range(1, OWNERS):
        acc = acc + a_ref[s].astype(F32)
    even = lax.rem(lax.axis_index("rep"), 2) == 0
    keep_ref[...] = jnp.where(even, acc[:32], acc[32:])
    send_ref[...] = jnp.where(even, acc[32:], acc[:32])


def last_kernel(own_ref, one_ref, two_ref, rest_ref, c_ref, slots_s):
    group = lax.axis_index("rep") // (2 * NEAR)
    for k, ref in enumerate((own_ref, one_ref, two_ref)):
        slots_s[lax.rem(group + 3 - k, 3)] = ref[...]
    total = (slots_s[0] + slots_s[1] + slots_s[2]).astype(BF)
    for o in range(OWNERS):
        c_ref[o, 0:32, :] = rest_ref[o]
        c_ref[o, 32:64, :] = total


def collect_kernel(cuts, index_ref, *refs):
    *in_refs, out_ref, acc_s = refs
    acc_s[...] = jnp.zeros_like(acc_s)

    def body(s, carry):
        for ref, pieces in zip(in_refs, cuts):
            for slot, at, to, rows in pieces:
                i = index_ref[2 * s + slot]
                acc_s[i, to : to + rows, :] += ref[s, at : at + rows, :].astype(F32)
        return carry

    lax.fori_loop(0, OWNERS, body, 0, unroll=4)
    for i in range(TRASH):
        out_ref[RB * i : RB * i + RB, :HALF] = acc_s[i, 0:32, :].astype(BF)
        out_ref[RB * i : RB * i + RB, HALF:] = acc_s[i, 32:64, :].astype(BF)


def unpack_kernel(mine_ref, other_ref, self_ref, inter_ref):
    even = lax.rem(lax.axis_index("rep"), 2) == 0
    for o in range(OWNERS):
        mine = mine_ref[o, 32:64, :].astype(F32)
        other = other_ref[o].astype(F32)
        a = jnp.where(even, mine, other)
        b = jnp.where(even, other, mine)
        rows = slice(8 * o, 8 * o + 8)
        for ref, value in ((self_ref, a), (inter_ref, b)):
            ref[1, rows, :HALF] = value[0:8]
            ref[1, rows, HALF:] = value[8:16]
            ref[0, rows, :HALF] = value[16:24]
            ref[0, rows, HALF:] = value[24:32]


def call(kernel, outs, in_specs, scratch=(), params=PARAMS, **cost):
    return pl.pallas_call(
        kernel,
        out_shape=[jax.ShapeDtypeStruct(s, d) for s, d in outs],
        in_specs=in_specs,
        out_specs=[VMEM] * len(outs),
        scratch_shapes=list(scratch),
        compiler_params=params,
        cost_estimate=pl.CostEstimate(transcendentals=0, **cost),
    )


def local(cotangent, pre_two, pre_one, message_two, message_one, users_zero, w_self, w_inter, adjacency, tile_user,
          counts, dest, item_block):
    users = cotangent.shape[0]
    reps = lax.axis_size("rep")
    z_chips = reps // 2
    swap = [(i, i ^ 1) for i in range(reps)]
    dest = dest.reshape(dest.shape[0])

    def from_z(x, source):
        return lax.ppermute(x, "rep", [(2 * source(z) + c, 2 * z + c) for z in range(z_chips) for c in range(2)])

    def to_owners(x):
        return lax.all_to_all(x, "owner", split_axis=0, concat_axis=0, tiled=True)

    def rows(n):
        return ((OWNERS, n, HALF), BF)

    user = ((users, FEAT), BF)
    both = ((2, FEAT, FEAT), F32)
    chunk = ((32, HALF), F32)
    ranks = [pltpu.SMEM((OWNERS,), jnp.int32)] * 2
    small = dict(flops=1_000_000, bytes_accessed=2 << 20)
    tile = dict(flops=140_000_000, bytes_accessed=2 << 20)
    dmsg2, dmsg1, user_grad, a = call(
        user_kernel,
        [user, user, user, rows(64)],
        [HBM] * 8,
        [pltpu.VMEM((users, FEAT), BF)] * 6 + [pltpu.VMEM((2, FEAT, FEAT), BF)] * 2
        + [pltpu.VMEM((users, FEAT), BF)] * 6 + [pltpu.SemaphoreType.DMA((8 + 6 * (users // BLK),))],
        params=WIDE, flops=900_000_000, bytes_accessed=6 << 20,
    )(cotangent, pre_two, pre_one, message_two, message_one, users_zero, w_self, w_inter)
    got_a = to_owners(a)

    two, index_rows = call(
        two_kernel, [((2, OWNERS, 64, HALF), BF), rows(8)], [SMEM] * 4 + [VMEM] * 2,
        ranks + [pltpu.SMEM((2 * OWNERS,), jnp.int32)], **tile,
    )(tile_user, counts, dest, item_block, adjacency, dmsg2)
    b, rest = call(
        one_kernel, [rows(232), rows(32)], [SMEM] * 3 + [VMEM] * 4,
        [pltpu.VMEM((2, OWNERS, 64, HALF), BF)] + ranks, **tile,
    )(tile_user, counts, dest, adjacency, dmsg1, two, index_rows)
    b, got_a = lax.optimization_barrier((b, got_a))
    got_b = to_owners(b)

    keep, send = call(chunk_kernel, [chunk] * 2, [VMEM], **small)(got_a)
    total = keep + lax.ppermute(send, "rep", swap)
    total = total + from_z(total, lambda z: z ^ 1)
    total = total + from_z(total, lambda z: z ^ 2)
    far = [from_z(total, lambda z, k=k: (z + z_chips - NEAR * k) % z_chips) for k in (1, 2)]
    (c,) = call(last_kernel, [rows(64)], [VMEM] * 4, [pltpu.VMEM((3, 32, HALF), F32)], **small)(total, *far, rest)
    c, got_b = lax.optimization_barrier((c, got_b))
    got_c = to_owners(c)

    index = got_b[:, 224:232:4, 0].astype(jnp.int32).reshape(2 * OWNERS)

    def collect(cuts, *arrays):
        return call(
            functools.partial(collect_kernel, cuts), [((OWNERS * RB, FEAT), BF)], [SMEM] + [VMEM] * len(arrays),
            [pltpu.VMEM((TRASH + 1, 64, HALF), F32)], **small,
        )(index, *arrays)[0]

    item_one = collect((((0, 0, 0, 64), (1, 64, 0, 64)),), got_b)
    got_c, item_one = lax.optimization_barrier((got_c, item_one))
    other = lax.ppermute(got_c[:, 32:64], "rep", swap)
    item_zero = collect((((0, 128, 0, 64), (1, 192, 0, 32)), ((1, 0, 32, 32),)), got_b, got_c)
    self_grad, inter_grad = call(unpack_kernel, [both] * 2, [VMEM] * 2, **small)(got_c, other)
    return user_grad, item_one, item_zero, self_grad, inter_grad


def solution(mesh):
    both = ("owner", "rep")
    rows = P(both, None)
    return jax.shard_map(
        local,
        mesh=mesh,
        in_specs=(rows,) * 6 + (P(), P(), P(both, None, None), P(both), P(both), rows, P(both)),
        out_specs=(rows, rows, rows, P(), P()),
        check_vma=False,
    )
```

```python
import functools

import functools

import jax
import jax.numpy as jnp
from jax import lax
from jax.experimental import pallas as pl
from jax.experimental.pallas import tpu as pltpu
from jax.sharding import PartitionSpec as P

BF = jnp.bfloat16
F32 = jnp.float32
SLOPE = 0.2
RB = 32
FEAT = 256
HALF = 128
BLK = 256
OWNERS = 32
TRASH = 32
NEAR = 4
VMEM = pl.BlockSpec(memory_space=pltpu.VMEM)
SMEM = pl.BlockSpec(memory_space=pltpu.SMEM)
HBM = pl.BlockSpec(memory_space=pltpu.HBM)
PARAMS = pltpu.CompilerParams(vmem_limit_bytes=12 * 1024 * 1024)
WIDE = pltpu.CompilerParams(vmem_limit_bytes=60 * 1024 * 1024)


def tdot(a, b):
    return lax.dot_general(a, b, (((0,), (0,)), ((), ())), preferred_element_type=F32)


def dot_t(a, b):
    return lax.dot_general(a, b, (((1,), (1,)), ((), ())), preferred_element_type=F32)


def user_kernel(*refs):
    ins, rest = refs[:8], refs[8:]
    dmsg2_ref, delta1_s, a_ref = rest[:3]
    bufs, sum2_s, prod2_s, delta2_s, sum1_s, prod1_s, sems = rest[3:11], *rest[11:]
    users = ins[0].shape[0]
    blocks = users // BLK
    weights = [pltpu.make_async_copy(ins[i], bufs[i], sems.at[i]) for i in (6, 7)]
    for copy in weights:
        copy.start()
    loads = []
    for b in range(blocks):
        rows = pl.ds(b * BLK, BLK)
        loads.append(
            [pltpu.make_async_copy(ins[i].at[rows], bufs[i].at[rows], sems.at[8 + 6 * b + i]) for i in range(6)]
        )
        for copy in loads[-1]:
            copy.start()
    cot, pre2, pre1, msg2, msg1, zero, ws, wi = bufs
    for copy in weights:
        copy.wait()
    for b in range(blocks):
        rows = pl.ds(b * BLK, BLK)
        for copy in loads[b]:
            copy.wait()
        one = pre1[rows, :].astype(F32)
        prev = jnp.where(one > 0, one, SLOPE * one).astype(BF).astype(F32)
        deltas = (cot[rows, :].astype(F32) * jnp.where(pre2[rows, :].astype(F32) > 0, 1.0, SLOPE)).astype(BF)
        msg = msg2[rows, :].astype(F32)
        delta2_s[rows, :] = deltas
        sum2_s[rows, :] = (msg + prev).astype(BF)
        prod2_s[rows, :] = (msg * prev).astype(BF)
        back_self = dot_t(deltas, ws[1])
        back_inter = dot_t(deltas, wi[1])
        dmsg2_ref[rows, :] = (back_self + back_inter * prev).astype(BF)
        dprev = back_self + back_inter * msg
        deltas = (dprev * jnp.where(one > 0, 1.0, SLOPE)).astype(BF)
        msg = msg1[rows, :].astype(F32)
        prev = zero[rows, :].astype(F32)
        delta1_s[rows, :] = deltas
        sum1_s[rows, :] = (msg + prev).astype(BF)
        prod1_s[rows, :] = (msg * prev).astype(BF)
    for at, (sum_s, prod_s, delta_s) in enumerate(((sum2_s, prod2_s, delta2_s), (sum1_s, prod1_s, delta1_s))):
        for half, left_s in enumerate((sum_s, prod_s)):
            grad = tdot(left_s[...], delta_s[...])
            first = 32 * half + 16 * at
            for o in range(OWNERS):
                part = grad[8 * o : 8 * o + 8, :]
                part = jnp.concatenate([part[:, :HALF], part[:, HALF:]], axis=0)
                a_ref[o, first : first + 16, :] = part.astype(BF)


def rank_blocks(dest_ref, rank_s, seen_s):
    for o in range(OWNERS):
        seen_s[o] = 0
    for j in range(dest_ref.shape[0]):
        o = dest_ref[j]
        rank_s[j] = seen_s[o]
        seen_s[o] = seen_s[o] + 1


def tile_terms(user_ref, count_ref, dest_ref, adj_ref, dmsg_ref, rank_s, out_ref):
    for t in range(adj_ref.shape[0]):
        start = pl.multiple_of(user_ref[t] * BLK, BLK)
        part = tdot(adj_ref[t], dmsg_ref[pl.ds(start, BLK), :])
        live = lax.broadcasted_iota(jnp.int32, part.shape, 0) < count_ref[t]
        part = jnp.where(live, part, 0.0).astype(BF)
        for b in range(part.shape[0] // RB):
            j = t * (part.shape[0] // RB) + b
            block = part[b * RB : (b + 1) * RB, :]
            out_ref[rank_s[j], dest_ref[j], 0:32, :] = block[:, :HALF]
            out_ref[rank_s[j], dest_ref[j], 32:64, :] = block[:, HALF:]


def two_kernel(user_ref, count_ref, dest_ref, item_ref, adj_ref, dmsg_ref, slots_ref, index_ref, rank_s, seen_s, tab_s):
    rank_blocks(dest_ref, rank_s, seen_s)
    for i in range(2 * OWNERS):
        tab_s[i] = TRASH
    for j in range(dest_ref.shape[0]):
        tab_s[2 * dest_ref[j] + rank_s[j]] = item_ref[j]
    slots_ref[...] = jnp.zeros_like(slots_ref)
    top = lax.broadcasted_iota(jnp.int32, (8, HALF), 0) < 4
    for o in range(OWNERS):
        index_ref[o] = jnp.where(top, tab_s[2 * o], tab_s[2 * o + 1]).astype(F32).astype(BF)
    tile_terms(user_ref, count_ref, dest_ref, adj_ref, dmsg_ref, rank_s, slots_ref)


def one_kernel(user_ref, count_ref, dest_ref, adj_ref, delta_ref, msg_ref, zero_ref, ws_ref, wi_ref, two_ref, index_ref,
               b_ref, rest_ref, user_grad_ref, slots_s, dmsg_ref, rank_s, seen_s):
    rank_blocks(dest_ref, rank_s, seen_s)
    for b in range(delta_ref.shape[0] // BLK):
        rows = pl.ds(b * BLK, BLK)
        back_self = dot_t(delta_ref[rows, :], ws_ref[0])
        back_inter = dot_t(delta_ref[rows, :], wi_ref[0])
        dmsg_ref[rows, :] = (back_self + back_inter * zero_ref[rows, :].astype(F32)).astype(BF)
        user_grad_ref[rows, :] = (back_self + back_inter * msg_ref[rows, :].astype(F32)).astype(BF)
    slots_s[...] = jnp.zeros_like(slots_s)
    tile_terms(user_ref, count_ref, dest_ref, adj_ref, dmsg_ref, rank_s, slots_s)
    for o in range(OWNERS):
        b_ref[o, 0:64, :] = two_ref[0, o]
        b_ref[o, 64:128, :] = two_ref[1, o]
        b_ref[o, 128:192, :] = slots_s[0, o]
        b_ref[o, 192:224, :] = slots_s[1, o, 0:32, :]
        b_ref[o, 224:232, :] = index_ref[o]
        rest_ref[o] = slots_s[1, o, 32:64, :]


def chunk_kernel(a_ref, keep_ref, send_ref):
    acc = a_ref[0].astype(F32)
    for s in range(1, OWNERS):
        acc = acc + a_ref[s].astype(F32)
    even = lax.rem(lax.axis_index("rep"), 2) == 0
    keep_ref[...] = jnp.where(even, acc[:32], acc[32:])
    send_ref[...] = jnp.where(even, acc[32:], acc[:32])


def last_kernel(own_ref, one_ref, two_ref, rest_ref, c_ref, slots_s):
    group = lax.axis_index("rep") // (2 * NEAR)
    for k, ref in enumerate((own_ref, one_ref, two_ref)):
        slots_s[lax.rem(group + 3 - k, 3)] = ref[...]
    total = (slots_s[0] + slots_s[1] + slots_s[2]).astype(BF)
    for o in range(OWNERS):
        c_ref[o, 0:32, :] = rest_ref[o]
        c_ref[o, 32:64, :] = total


def collect_kernel(cuts, index_ref, *refs):
    *in_refs, out_ref, acc_s = refs
    acc_s[...] = jnp.zeros_like(acc_s)

    def body(s, carry):
        for ref, pieces in zip(in_refs, cuts):
            for slot, at, to, rows in pieces:
                i = index_ref[2 * s + slot]
                acc_s[i, to : to + rows, :] += ref[s, at : at + rows, :].astype(F32)
        return carry

    lax.fori_loop(0, OWNERS, body, 0, unroll=4)
    for i in range(TRASH):
        out_ref[RB * i : RB * i + RB, :HALF] = acc_s[i, 0:32, :].astype(BF)
        out_ref[RB * i : RB * i + RB, HALF:] = acc_s[i, 32:64, :].astype(BF)


def unpack_kernel(mine_ref, other_ref, self_ref, inter_ref):
    even = lax.rem(lax.axis_index("rep"), 2) == 0
    for o in range(OWNERS):
        mine = mine_ref[o, 32:64, :].astype(F32)
        other = other_ref[o].astype(F32)
        a = jnp.where(even, mine, other)
        b = jnp.where(even, other, mine)
        rows = slice(8 * o, 8 * o + 8)
        for ref, value in ((self_ref, a), (inter_ref, b)):
            ref[1, rows, :HALF] = value[0:8]
            ref[1, rows, HALF:] = value[8:16]
            ref[0, rows, :HALF] = value[16:24]
            ref[0, rows, HALF:] = value[24:32]


def call(kernel, outs, in_specs, scratch=(), params=PARAMS, **cost):
    return pl.pallas_call(
        kernel,
        out_shape=[jax.ShapeDtypeStruct(s, d) for s, d in outs],
        in_specs=in_specs,
        out_specs=[VMEM] * len(outs),
        scratch_shapes=list(scratch),
        compiler_params=params,
        cost_estimate=pl.CostEstimate(transcendentals=0, **cost),
    )


def local(cotangent, pre_two, pre_one, message_two, message_one, users_zero, w_self, w_inter, adjacency, tile_user,
          counts, dest, item_block):
    users = cotangent.shape[0]
    reps = lax.axis_size("rep")
    z_chips = reps // 2
    swap = [(i, i ^ 1) for i in range(reps)]
    dest = dest.reshape(dest.shape[0])

    def from_z(x, source):
        return lax.ppermute(x, "rep", [(2 * source(z) + c, 2 * z + c) for z in range(z_chips) for c in range(2)])

    def to_owners(x):
        return lax.all_to_all(x, "owner", split_axis=0, concat_axis=0, tiled=True)

    def rows(n):
        return ((OWNERS, n, HALF), BF)

    user = ((users, FEAT), BF)
    both = ((2, FEAT, FEAT), F32)
    chunk = ((32, HALF), F32)
    ranks = [pltpu.SMEM((OWNERS,), jnp.int32)] * 2
    small = dict(flops=1_000_000, bytes_accessed=2 << 20)
    tile = dict(flops=140_000_000, bytes_accessed=2 << 20)
    dmsg2, delta1, a = call(
        user_kernel,
        [user, user, rows(64)],
        [HBM] * 8,
        [pltpu.VMEM((users, FEAT), BF)] * 6 + [pltpu.VMEM((2, FEAT, FEAT), BF)] * 2
        + [pltpu.VMEM((users, FEAT), BF)] * 5 + [pltpu.SemaphoreType.DMA((8 + 6 * (users // BLK),))],
        params=WIDE, flops=900_000_000, bytes_accessed=6 << 20,
    )(cotangent, pre_two, pre_one, message_two, message_one, users_zero, w_self, w_inter)
    got_a = to_owners(a)

    two, index_rows = call(
        two_kernel, [((2, OWNERS, 64, HALF), BF), rows(8)], [SMEM] * 4 + [VMEM] * 2,
        ranks + [pltpu.SMEM((2 * OWNERS,), jnp.int32)], **tile,
    )(tile_user, counts, dest, item_block, adjacency, dmsg2)
    b, rest, user_grad = call(
        one_kernel, [rows(232), rows(32), user], [SMEM] * 3 + [VMEM] * 8,
        [pltpu.VMEM((2, OWNERS, 64, HALF), BF), pltpu.VMEM((users, FEAT), BF)] + ranks, **tile,
    )(tile_user, counts, dest, adjacency, delta1, message_one, users_zero, w_self, w_inter, two, index_rows)
    b, got_a = lax.optimization_barrier((b, got_a))
    got_b = to_owners(b)

    keep, send = call(chunk_kernel, [chunk] * 2, [VMEM], **small)(got_a)
    total = keep + lax.ppermute(send, "rep", swap)
    total = total + from_z(total, lambda z: z ^ 1)
    total = total + from_z(total, lambda z: z ^ 2)
    far = [from_z(total, lambda z, k=k: (z + z_chips - NEAR * k) % z_chips) for k in (1, 2)]
    (c,) = call(last_kernel, [rows(64)], [VMEM] * 4, [pltpu.VMEM((3, 32, HALF), F32)], **small)(total, *far, rest)
    c, got_b = lax.optimization_barrier((c, got_b))
    got_c = to_owners(c)

    index = got_b[:, 224:232:4, 0].astype(jnp.int32).reshape(2 * OWNERS)

    def collect(cuts, *arrays):
        return call(
            functools.partial(collect_kernel, cuts), [((OWNERS * RB, FEAT), BF)], [SMEM] + [VMEM] * len(arrays),
            [pltpu.VMEM((TRASH + 1, 64, HALF), F32)], **small,
        )(index, *arrays)[0]

    item_one = collect((((0, 0, 0, 64), (1, 64, 0, 64)),), got_b)
    got_c, item_one = lax.optimization_barrier((got_c, item_one))
    other = lax.ppermute(got_c[:, 32:64], "rep", swap)
    item_zero = collect((((0, 128, 0, 64), (1, 192, 0, 32)), ((1, 0, 32, 32),)), got_b, got_c)
    self_grad, inter_grad = call(unpack_kernel, [both] * 2, [VMEM] * 2, **small)(got_c, other)
    return user_grad, item_one, item_zero, self_grad, inter_grad


def solution(mesh):
    both = ("owner", "rep")
    rows = P(both, None)
    return jax.shard_map(
        local,
        mesh=mesh,
        in_specs=(rows,) * 6 + (P(), P(), P(both, None, None), P(both), P(both), rows, P(both)),
        out_specs=(rows, rows, rows, P(), P()),
        check_vma=False,
    )
```
